256 devices in a mesh: ctx: 32 (over z, y_hi, core), kv: 8 (over x, y_lo).
Axes of the slice: x: 4, y: 4 (y_hi: 2, y_lo: 2; y = y_hi * 2 + y_lo), z: 8, core: 2. Of those that a mesh axis runs over, the one named last changes fastest.
Arguments:
- queries: bfloat16 [1024, 64, 128], P('ctx', 'kv'), may hold values from -64 to 64
- new_keys: bfloat16 [1024, 8, 128], P('ctx', 'kv'), may hold values from -8 to 8
- new_values: bfloat16 [1024, 8, 128], P('ctx', 'kv'), may hold values from -6 to 6
- key_cache: bfloat16 [262144, 8, 128], P('ctx', 'kv'), may hold values from -6 to 6
- value_cache: bfloat16 [262144, 8, 128], P('ctx', 'kv'), may hold values from -6 to 6
- page_slots: int32 [32, 32, 8], P('ctx'), may hold values from 0 to 63, as said below
- page_counts: int32 [32, 32], P('ctx'), may hold values from 0 to 8, as said below
- out_weight: bfloat16 [8192, 8192], P('kv', 'ctx'), may hold values from -1.5 to 1.5
Outputs:
- layer_out: bfloat16 [1024, 8192], P('kv', 'ctx')
The draws below stay inside these ranges and needn't reach their ends.
Inputs may be any that keep to these rules, and one draw needn't show every extreme that they name: page_counts[s, b] of the 8 slots of page_slots[s, b] hold selected pages; for every block b some shard s has exactly 8. The 8 entries of page_slots[s, b] are distinct pages of shard s; only the first page_counts[s, b] are selected, the others are not read.
All inputs are finite; a program needn't handle non-finite values.
Results may differ from the reference program's by a relative error of at most 0.019.
Values may be sent and summed in bfloat16 or wider, within the bound.
A program may use at most 64 MiB of HBM per device.

```python
import jax
import jax.numpy as jnp
from jax import lax

HEAD = 128
Q_HEADS = 64
KV_HEADS = 8
MODEL = 8192
GROUP = 8
PAGE = 128
QTOK = 32
PAGES_DEV = 64
MOST = 8
QBLOCKS = 32
SHARDS = 32
NEW = 1024
CACHE = 262144


def shared_parts(key):
    base = jnp.clip(jax.random.normal(jax.random.fold_in(key, 11), (NEW, KV_HEADS, HEAD), jnp.float32), -4.0, 4.0)
    return base


def draw_new_keys(key, part):
    base = shared_parts(key)
    return base.astype(jnp.bfloat16)


def draw_queries(key, part):
    key = jax.random.fold_in(key, 2)
    drawn = 1.5 * jnp.clip(jax.random.normal(key, (NEW, Q_HEADS, HEAD), jnp.float32), -4.0, 4.0)
    return drawn.astype(jnp.bfloat16)


def draw_page_counts(key, part):
    key = jax.random.fold_in(key, 3)
    light_counts = jax.random.randint(jax.random.fold_in(key, 1), (SHARDS, QBLOCKS), 0, MOST // 2 + 1)
    busiest = jax.random.randint(jax.random.fold_in(key, 2), (QBLOCKS,), 0, SHARDS)
    shard_ids = jnp.arange(SHARDS, dtype=jnp.int32)[:, None]
    return jnp.where(shard_ids == busiest[None, :], MOST, light_counts).astype(jnp.int32)


def draw_page_slots(key, part):
    key = jax.random.fold_in(key, 4)
    random_bits = jax.random.randint(key, (SHARDS, QBLOCKS, PAGES_DEV), 0, 1 << 20)
    ranked = random_bits * PAGES_DEV + jnp.arange(PAGES_DEV, dtype=jnp.int32)
    shuffled = jnp.argsort(ranked, axis=-1, stable=True)
    return shuffled[..., :MOST].astype(jnp.int32)


def steps_of(rng, extent, split, least, largest):
    def one(axis_at, blocks):
        steps = jax.random.uniform(jax.random.fold_in(jax.random.fold_in(rng, 6), axis_at), (blocks,), jnp.float32, least / len(split), largest / len(split))
        return jnp.repeat(jnp.exp(steps), extent[axis_at] // blocks).reshape((-1,) + (1,) * (len(extent) - axis_at - 1))

    factor_of = one(*split[0])
    for cut in split[1:]:
        factor_of = factor_of * one(*cut)
    return factor_of


def bell_draw(rng, dims, scale, bound, shards=(), held_as=jnp.bfloat16):
    gain = steps_of(rng, dims, shards, -0.22, 0.18) if shards else 1.0
    array = jax.random.normal(rng, dims, jnp.float32) * scale * gain
    return jnp.minimum(jnp.maximum(array, -bound), bound).astype(held_as)


def setup_inputs(seed: int = 0) -> dict:
    streams_of = jax.random.split(jax.random.key(seed), 9)
    return {
        "queries": draw_queries(jax.random.fold_in(streams_of[8], 71), 0),
        "new_keys": draw_new_keys(jax.random.fold_in(streams_of[8], 71), 0),
        "new_values": bell_draw(streams_of[2], (NEW, KV_HEADS, HEAD), 1.0, 6.0, ((0, 32), (1, 8))),
        "key_cache": bell_draw(streams_of[3], (CACHE, KV_HEADS, HEAD), 1.0, 6.0, ((0, 32), (1, 8))),
        "value_cache": bell_draw(streams_of[4], (CACHE, KV_HEADS, HEAD), 1.0, 6.0, ((0, 32), (1, 8))),
        "page_slots": draw_page_slots(jax.random.fold_in(streams_of[8], 71), 0),
        "page_counts": draw_page_counts(jax.random.fold_in(streams_of[8], 71), 0),
        "out_weight": bell_draw(streams_of[7], (MODEL, MODEL), 16 ** -0.5, 1.5, ((0, 8), (1, 32))),
    }


NEG_FILL = -1.0e30


def softmax_part(query_rows, key_rows, value_rows, live_mask):
    scores = jnp.einsum("tkgd,nkd->tkgn", query_rows, key_rows) * (HEAD ** -0.5)
    widened = live_mask[:, None, None, :]
    highest = jnp.max(jnp.where(widened, scores, NEG_FILL), axis=-1)
    weights = jnp.where(widened, jnp.exp(scores - highest[..., None]), 0.0).astype(jnp.bfloat16)
    wide_weights = weights.astype(jnp.float32)
    totals = jnp.sum(wide_weights, axis=-1)
    summed = jnp.einsum("tkgn,nkd->tkgd", wide_weights, value_rows)
    return summed, highest, totals


def reference(queries, new_keys, new_values, key_cache, value_cache, page_slots, page_counts, out_weight):
    key_pages = key_cache.reshape(SHARDS * PAGES_DEV, PAGE, KV_HEADS, HEAD)
    value_pages = value_cache.reshape(SHARDS * PAGES_DEV, PAGE, KV_HEADS, HEAD)
    fresh_keys = new_keys.astype(jnp.float32)
    fresh_values = new_values.astype(jnp.float32)
    positions = jnp.arange(NEW, dtype=jnp.int32)

    def one_block(block_index):
        first_row = (block_index * QTOK).astype(jnp.int32)
        query_rows = lax.dynamic_slice_in_dim(queries, first_row, QTOK, 0)
        query_rows = query_rows.astype(jnp.float32).reshape(QTOK, KV_HEADS, GROUP, HEAD)

        def one_shard(shard_index):
            page_list = page_slots[shard_index, block_index] + shard_index * PAGES_DEV
            key_rows = jnp.take(key_pages, page_list, axis=0).reshape(MOST * PAGE, KV_HEADS, HEAD)
            value_rows = jnp.take(value_pages, page_list, axis=0).reshape(MOST * PAGE, KV_HEADS, HEAD)
            live_pages = jnp.arange(MOST, dtype=jnp.int32) < page_counts[shard_index, block_index]
            live_mask = jnp.broadcast_to(jnp.repeat(live_pages, PAGE)[None, :], (QTOK, MOST * PAGE))
            return softmax_part(query_rows, key_rows.astype(jnp.float32), value_rows.astype(jnp.float32), live_mask)

        shard_sums, shard_tops, shard_totals = lax.map(one_shard, jnp.arange(SHARDS, dtype=jnp.int32))
        query_pos = first_row + jnp.arange(QTOK, dtype=jnp.int32)
        causal = positions[None, :] <= query_pos[:, None]
        new_sum, new_top, new_total = softmax_part(query_rows, fresh_keys, fresh_values, causal)
        highest = jnp.maximum(jnp.max(shard_tops, axis=0), new_top)
        cache_scale = jnp.exp(shard_tops - highest[None])
        new_scale = jnp.exp(new_top - highest)
        summed = jnp.sum(shard_sums * cache_scale[..., None], axis=0) + new_sum * new_scale[..., None]
        totals = jnp.sum(shard_totals * cache_scale, axis=0) + new_total * new_scale
        attention = (summed / totals[..., None]).astype(jnp.bfloat16)
        return attention.reshape(QTOK, MODEL)

    attention_rows = lax.map(one_block, jnp.arange(QBLOCKS, dtype=jnp.int32)).reshape(NEW, MODEL)
    return jnp.dot(attention_rows, out_weight, preferred_element_type=jnp.float32).astype(jnp.bfloat16)
```

```python
import jax
import jax.numpy as jnp
from jax import lax
from jax.experimental import pallas as pl
from jax.experimental.pallas import tpu as pltpu
from jax.sharding import PartitionSpec as P

PAGE = 128
HEAD = 128
ROWS = 256
MSG = 144
QTOK = 32
ZS = 8
BLOCKS = 32
NEG_FILL = -1e30
LOG2E = 1.4426950408889634
FACTOR = HEAD ** (-0.5) * LOG2E
MIB = 1 << 20
MESH = pl.DeviceIdType.MESH

LEN = ((4, 3), (3, 4))
WAYS = (1, -1)


class Place:
    def __init__(self):
        self.me = lax.axis_index("ctx")
        self.kv = lax.axis_index("kv")
        self.z = self.me // 4
        self.yh = (self.me % 4) // 2
        self.core = self.me % 2

    def block(self, dz, chain, other_core=False):
        z = lax.rem(self.z + dz + ZS, ZS)
        yh = 1 - self.yh if chain else self.yh
        core = 1 - self.core if other_core else self.core
        return z * 4 + yh * 2 + core


def remote(src, dst, send, recv, ctx):
    return pltpu.make_async_remote_copy(
        src_ref=src, dst_ref=dst, send_sem=send, recv_sem=recv,
        device_id={"ctx": ctx}, device_id_type=MESH,
    )


def greet(place, with_kv):
    barrier = pltpu.get_barrier_semaphore()
    peers = (place.block(1, 0), place.block(-1, 0), place.block(0, 1), place.block(0, 0, True))
    for peer in peers:
        pl.semaphore_signal(barrier, inc=1, device_id={"ctx": peer}, device_id_type=MESH)
    count = len(peers)
    if with_kv:
        for off in range(1, ZS):
            other = lax.rem(place.kv + off, ZS)
            pl.semaphore_signal(barrier, inc=1, device_id={"kv": other}, device_id_type=MESH)
        count += ZS - 1
    pl.semaphore_wait(barrier, count)


def pair_slot(dz, chain):
    return (dz % ZS) * 2 + chain


def gather_blocks(place, slots, zsend, zrecv, csend, crecv, ysem, planes=None):
    started = []

    def send_z(dz, chain, way, step):
        b = place.block(dz, chain)
        copy = remote(
            slots.at[b], slots.at[b], zsend.at[chain, way, step - 1], zrecv.at[chain, way, step - 1],
            place.block(WAYS[way], 0),
        )
        copy.start()
        started.append(copy)

    def send_core(dz, chain):
        b = place.block(dz, chain)
        k = pair_slot(dz, chain)
        copy = remote(slots.at[b], slots.at[b], csend.at[k], crecv.at[k], place.block(0, 0, True))
        copy.start()
        started.append(copy)

    def wait_core(dz, chain):
        b = place.block(dz, chain, True)
        k = pair_slot(dz, chain)
        remote(slots.at[b], slots.at[b], csend.at[k], crecv.at[k], place.block(0, 0, True)).wait_recv()

    def plane(dz):
        for chain in (0, 1):
            wait_core(dz, chain)
        if planes is not None:
            planes(dz)

    own = place.block(0, 0)
    partner = place.block(0, 1)
    y_copy = remote(slots.at[own], slots.at[own], ysem.at[0], ysem.at[1], partner)
    y_copy.start()
    started.append(y_copy)
    send_z(0, 0, 0, 1)
    send_z(0, 0, 1, 1)
    send_core(0, 0)
    remote(slots.at[partner], slots.at[partner], ysem.at[0], ysem.at[1], partner).wait_recv()
    send_z(0, 1, 0, 1)
    send_z(0, 1, 1, 1)
    send_core(0, 1)
    for step in range(1, 5):
        for chain in (0, 1):
            for way in (0, 1):
                if LEN[chain][way] < step:
                    continue
                dz = -step * WAYS[way]
                b = place.block(dz, chain)
                remote(
                    slots.at[b], slots.at[b], zsend.at[chain, way, step - 1], zrecv.at[chain, way, step - 1],
                    place.block(WAYS[way], 0),
                ).wait_recv()
                if step < LEN[chain][way]:
                    send_z(dz, chain, way, step + 1)
                send_core(dz, chain)
        if step == 1:
            plane(0)
        else:
            plane(step - 1)
            plane(1 - step)
    plane(4)
    for copy in started:
        copy.wait_send()


GATHER_SEMS = [
    pltpu.SemaphoreType.DMA((2, 2, 4)),
    pltpu.SemaphoreType.DMA((2, 2, 4)),
    pltpu.SemaphoreType.DMA((16,)),
    pltpu.SemaphoreType.DMA((16,)),
    pltpu.SemaphoreType.DMA((2,)),
]


def gather_kernel(q_ref, v_ref, nv_ref, g_ref, vt_ref, nvt_ref, *sems):
    place = Place()
    greet(place, False)
    g_ref[place.me] = q_ref[...]

    def turn(i, _):
        at = pl.multiple_of(i * PAGE, PAGE)
        vt_ref[i, 0:HEAD, :] = v_ref[pl.ds(at, PAGE), :].T
        vt_ref[i, HEAD:MSG, :] = jnp.ones((MSG - HEAD, PAGE), jnp.bfloat16)
        return 0

    count = v_ref.shape[0] // PAGE
    lax.fori_loop(0, count, turn, 0)
    nvt_ref[0:HEAD, :] = nv_ref[...].T
    nvt_ref[HEAD:MSG, :] = jnp.ones((MSG - HEAD, QTOK), jnp.bfloat16)
    gather_blocks(place, g_ref, *sems)


def gather_queries(q, v, nv):
    pages = v.shape[0] // PAGE
    return pl.pallas_call(
        gather_kernel,
        out_shape=(
            jax.ShapeDtypeStruct((BLOCKS, ROWS, HEAD), jnp.bfloat16),
            jax.ShapeDtypeStruct((pages, MSG, PAGE), jnp.bfloat16),
            jax.ShapeDtypeStruct((MSG, QTOK), jnp.bfloat16),
        ),
        in_specs=[pl.BlockSpec(memory_space=pltpu.VMEM)] * 3,
        out_specs=[pl.BlockSpec(memory_space=pltpu.VMEM)] * 3,
        scratch_shapes=GATHER_SEMS,
        compiler_params=pltpu.CompilerParams(
            collective_id=0, has_side_effects=True, vmem_limit_bytes=20 * MIB
        ),
        name="gather_queries",
    )(q, v, nv)


def write_message(ref, top, total, sums):
    ref[0:HEAD, :] = sums.astype(jnp.bfloat16)
    high = total.astype(jnp.bfloat16).astype(jnp.float32)
    low = total - high
    row = lax.broadcasted_iota(jnp.int32, (MSG - HEAD, ROWS), 0)
    stats = jnp.where(row == 0, top, jnp.where(row == 1, high, jnp.where(row == 2, low, 0.0)))
    ref[HEAD:MSG, :] = stats.astype(jnp.bfloat16)


def merged(refs):
    tops, totals = [], []
    for ref in refs:
        stats = ref[HEAD:MSG, :].astype(jnp.float32)
        tops.append(stats[0:1, :])
        totals.append(stats[1:2, :] + stats[2:3, :])
    top = tops[0]
    for other in tops[1:]:
        top = jnp.maximum(top, other)
    total = None
    sums = None
    for ref, t, n in zip(refs, tops, totals):
        scale = jnp.exp2(t - top)
        piece = ref[0:HEAD, :].astype(jnp.float32) * scale
        total = n * scale if total is None else total + n * scale
        sums = piece if sums is None else sums + piece
    return top, total, sums


def partial_kernel(slots_ref, counts_ref, q_ref, k_ref, vt_ref, nk_ref, nvt_ref, out_ref):
    shard = lax.axis_index("ctx")
    contract = (((1,), (1,)), ((), ()))

    def one(b, _):
        count = counts_ref[b]

        def case(n):
            def run():
                q = q_ref[b]
                new = lax.dot_general(nk_ref[...], q, contract, preferred_element_type=jnp.float32)
                key = lax.broadcasted_iota(jnp.int32, (QTOK, ROWS), 0)
                token = lax.broadcasted_iota(jnp.int32, (QTOK, ROWS), 1) // (ROWS // QTOK)
                live = key + shard * QTOK <= token + b * QTOK
                new = jnp.where(live, new, NEG_FILL)
                scores = []
                pages = []
                top = jnp.max(new, axis=0, keepdims=True)
                for j in range(n):
                    page = slots_ref[b, j]
                    pages.append(page)
                    at = pl.multiple_of(page * PAGE, PAGE)
                    scores.append(
                        lax.dot_general(
                            k_ref[pl.ds(at, PAGE), :], q, contract, preferred_element_type=jnp.float32
                        )
                    )
                if n:
                    most = scores[0]
                    for other in scores[1:]:
                        most = jnp.maximum(most, other)
                    top = jnp.maximum(top, jnp.max(most, axis=0, keepdims=True))
                top = jnp.maximum(top * FACTOR, NEG_FILL).astype(jnp.bfloat16).astype(jnp.float32)
                weights = jnp.where(live, jnp.exp2(new * FACTOR - top), 0.0).astype(jnp.bfloat16)
                both = jnp.dot(nvt_ref[...], weights, preferred_element_type=jnp.float32)
                if n:
                    weights = [jnp.exp2(s * FACTOR - top).astype(jnp.bfloat16) for s in scores]
                    values = [vt_ref[page] for page in pages]
                    both = both + jnp.dot(
                        jnp.concatenate(values, axis=1) if n > 1 else values[0],
                        jnp.concatenate(weights, axis=0) if n > 1 else weights[0],
                        preferred_element_type=jnp.float32,
                    )
                write_message(out_ref.at[b], top, both[HEAD : HEAD + 1, :], both[0:HEAD, :])

            return run

        for n in range(9):
            pl.when(count == n)(case(n))
        return 0

    lax.fori_loop(0, BLOCKS, one, 0)


def partials(slots, counts, q, k, vt, nk, nvt):
    return pl.pallas_call(
        partial_kernel,
        out_shape=jax.ShapeDtypeStruct((BLOCKS, MSG, ROWS), jnp.bfloat16),
        in_specs=[pl.BlockSpec(memory_space=pltpu.SMEM)] * 2 + [pl.BlockSpec(memory_space=pltpu.VMEM)] * 5,
        out_specs=pl.BlockSpec(memory_space=pltpu.VMEM),
        compiler_params=pltpu.CompilerParams(vmem_limit_bytes=24 * MIB),
        name="partials",
    )(slots, counts, q, k, vt, nk, nvt)


def finish_kernel(
    p_ref, w_ref, out_ref,
    c_buf, t_buf, r_buf, y_buf, turned, a_buf, mine_buf, kv_buf,
    c_send, c_recv, z_send, z_recv, y_sem, kv_send, kv_recv, *sems,
):
    place = Place()
    greet(place, True)
    started = []
    sibling = place.block(0, 0, True)

    order = [(dz, chain) for far in (4, 3, 2, 1) for dz in ((far, -far) if far < 4 else (4,)) for chain in (0, 1)]
    order += [(0, 1), (0, 0)]
    for dz, chain in order:
        k = pair_slot(dz, chain)
        copy = remote(p_ref.at[place.block(dz, chain, True)], c_buf.at[k], c_send.at[k], c_recv.at[k], sibling)
        copy.start()
        started.append(copy)

    def local(dz, chain):
        k = pair_slot(dz, chain)
        b = place.block(dz, chain)
        remote(p_ref.at[b], c_buf.at[k], c_send.at[k], c_recv.at[k], sibling).wait_recv()
        return [p_ref.at[b], c_buf.at[k]]

    def z_copy(chain, way, step):
        at = chain, way, step - 1
        return remote(t_buf.at[at], r_buf.at[at], z_send.at[at], z_recv.at[at], place.block(WAYS[way], 0))

    for step in range(1, 5):
        for chain in (0, 1):
            for way in (0, 1):
                length = LEN[chain][1 - way]
                if step > length:
                    continue
                parts = local(WAYS[way] * (length + 1 - step), chain)
                if step > 1:
                    z_copy(chain, way, step - 1).wait_recv()
                    parts.append(r_buf.at[chain, way, step - 2])
                write_message(t_buf.at[chain, way, step - 1], *merged(parts))
                copy = z_copy(chain, way, step)
                copy.start()
                started.append(copy)

    def home(chain):
        parts = local(0, chain)
        for way in (0, 1):
            length = LEN[chain][1 - way]
            z_copy(chain, way, length).wait_recv()
            parts.append(r_buf.at[chain, way, length - 1])
        return parts

    write_message(y_buf.at[0], *merged(home(1)))
    y_copy = remote(y_buf.at[0], y_buf.at[1], y_sem.at[0], y_sem.at[1], place.block(0, 1))
    y_copy.start()
    parts = home(0)
    y_copy.wait()
    _, total, sums = merged(parts + [y_buf.at[1]])
    turned[...] = (sums * (1.0 / total)).T
    heads = ROWS // QTOK
    for g in range(heads):
        a_buf[place.me, :, g * HEAD : (g + 1) * HEAD] = turned[pl.ds(g, QTOK, stride=heads), :].astype(jnp.bfloat16)

    def kv_copy(target, step):
        return pltpu.make_async_remote_copy(
            src_ref=mine_buf.at[target], dst_ref=kv_buf.at[place.kv],
            send_sem=kv_send.at[target], recv_sem=kv_recv.at[place.kv],
            device_id={"kv": target}, device_id_type=MESH,
        )

    def project(dz):
        plane = lax.rem(place.z + dz + ZS, ZS)
        rows = a_buf[pl.ds(pl.multiple_of(plane * 4, 4), 4)].reshape(4 * QTOK, a_buf.shape[2])
        mine_buf[plane] = jnp.dot(rows, w_ref[...], preferred_element_type=jnp.float32).astype(jnp.bfloat16)

        @pl.when(plane != place.kv)
        def _():
            kv_copy(plane, dz).start()

    gather_blocks(place, a_buf, *sems, planes=project)

    total = mine_buf[place.kv].astype(jnp.float32)
    for off in range(1, ZS):
        other = lax.rem(place.kv + off, ZS)
        pltpu.make_async_remote_copy(
            src_ref=mine_buf.at[other], dst_ref=kv_buf.at[other],
            send_sem=kv_send.at[other], recv_sem=kv_recv.at[other],
            device_id={"kv": other}, device_id_type=MESH,
        ).wait()
        total = total + kv_buf[other].astype(jnp.float32)
    out_ref[...] = total.astype(jnp.bfloat16)
    for copy in started:
        copy.wait_send()


def finish(p, w):
    width = w.shape[1]
    return pl.pallas_call(
        finish_kernel,
        out_shape=jax.ShapeDtypeStruct((4 * QTOK, width), jnp.bfloat16),
        in_specs=[pl.BlockSpec(memory_space=pltpu.VMEM)] * 2,
        out_specs=pl.BlockSpec(memory_space=pltpu.VMEM),
        scratch_shapes=[
            pltpu.VMEM((16, MSG, ROWS), jnp.bfloat16),
            pltpu.VMEM((2, 2, 4, MSG, ROWS), jnp.bfloat16),
            pltpu.VMEM((2, 2, 4, MSG, ROWS), jnp.bfloat16),
            pltpu.VMEM((2, MSG, ROWS), jnp.bfloat16),
            pltpu.VMEM((ROWS, HEAD), jnp.float32),
            pltpu.VMEM((BLOCKS, QTOK, w.shape[0]), jnp.bfloat16),
            pltpu.VMEM((ZS, 4 * QTOK, width), jnp.bfloat16),
            pltpu.VMEM((ZS, 4 * QTOK, width), jnp.bfloat16),
            pltpu.SemaphoreType.DMA((16,)),
            pltpu.SemaphoreType.DMA((16,)),
            pltpu.SemaphoreType.DMA((2, 2, 4)),
            pltpu.SemaphoreType.DMA((2, 2, 4)),
            pltpu.SemaphoreType.DMA((2,)),
            pltpu.SemaphoreType.DMA((ZS,)),
            pltpu.SemaphoreType.DMA((ZS,)),
        ]
        + GATHER_SEMS,
        compiler_params=pltpu.CompilerParams(
            collective_id=1, has_side_effects=True, vmem_limit_bytes=24 * MIB
        ),
        name="finish",
    )(p, w)


def body(queries, new_keys, new_values, key_cache, value_cache, page_slots, page_counts, out_weight):
    q = queries.reshape(ROWS, HEAD)
    nk = new_keys.reshape(QTOK, HEAD)
    nv = new_values.reshape(QTOK, HEAD)
    k = key_cache.reshape(-1, HEAD)
    v = value_cache.reshape(-1, HEAD)
    g, vt, nvt = gather_queries(q, v, nv)
    p = partials(page_slots[0], page_counts[0], g, k, vt, nk, nvt)
    return finish(p, out_weight)


def solution(mesh):
    placed = (
        P("ctx", "kv", None),
        P("ctx", "kv", None),
        P("ctx", "kv", None),
        P("ctx", "kv", None),
        P("ctx", "kv", None),
        P("ctx", None, None),
        P("ctx", None),
        P("kv", "ctx"),
    )
    return jax.shard_map(
        body, mesh=mesh, in_specs=placed, out_specs=P("kv", "ctx"), check_vma=False
    )
```

```python
import jax
import jax.numpy as jnp
from jax import lax
from jax.experimental import pallas as pl
from jax.experimental.pallas import tpu as pltpu
from jax.sharding import PartitionSpec as P

PAGE = 128
HEAD = 128
QTOK = 32
GROUP = 8
HALF = 128
MSG = 144
ZS = 8
COLUMN = 16
MOST = 8
NEG_FILL = -1e30
FACTOR = HEAD ** (-0.5) * 1.4426950408889634
MIB = 1 << 20
MESH = pl.DeviceIdType.MESH
BF16 = jnp.bfloat16
F32 = jnp.float32

LEN = ((4, 3), (3, 4))
WAYS = (1, -1)
HALVES = (0, 1)


class Place:
    def __init__(self):
        self.me = lax.axis_index("ctx")
        self.kv = lax.axis_index("kv")
        self.z = self.me // 4
        self.yh = (self.me % 4) // 2
        self.core = self.me % 2
        self.above = self.block(1, 0)
        self.below = self.block(-1, 0)
        self.partner = self.block(0, 1)
        self.sibling = self.z * 4 + self.yh * 2 + 1 - self.core

    def slot(self, dz, chain):
        z = lax.rem(self.z + dz + ZS, ZS)
        return z * 2 + (1 - self.yh if chain else self.yh)

    def block(self, dz, chain):
        return self.slot(dz, chain) * 2 + self.core

    def along(self, way):
        return self.below if way else self.above


def remote(src, dst, send, recv, **where):
    return pltpu.make_async_remote_copy(
        src_ref=src, dst_ref=dst, send_sem=send, recv_sem=recv, device_id=where, device_id_type=MESH
    )


def greet(wheres):
    barrier = pltpu.get_barrier_semaphore()
    for where in wheres:
        pl.semaphore_signal(barrier, inc=1, device_id=where, device_id_type=MESH)
    pl.semaphore_wait(barrier, len(wheres))


class Gather:
    def __init__(self, place, slots, own, z_send, z_recv, y_send, y_recv):
        self.place, self.slots, self.own = place, slots, own
        self.sems = z_send, z_recv, y_send, y_recv
        self.started = []

    def z_copy(self, chain, way, step, half, src=None):
        here = self.slots.at[self.place.slot(-(step - 1) * WAYS[way], chain), half]
        at = chain, way, step - 1, half
        return remote(
            here if src is None else src, here, self.sems[0].at[at], self.sems[1].at[at], ctx=self.place.along(way)
        )

    def z_start(self, *args, **more):
        copy = self.z_copy(*args, **more)
        copy.start()
        self.started.append(copy)

    def z_wait(self, chain, way, step, half):
        there = self.slots.at[self.place.slot(-step * WAYS[way], chain), half]
        at = chain, way, step - 1, half
        remote(there, there, self.sems[0].at[at], self.sems[1].at[at], ctx=self.place.along(way)).wait_recv()

    def start(self, half):
        src = self.own(half)
        copy = remote(
            src, self.slots.at[self.place.slot(0, 0), half], self.sems[2].at[half], self.sems[3].at[half],
            ctx=self.place.partner,
        )
        copy.start()
        self.started.append(copy)
        for way in (0, 1):
            self.z_start(0, way, 1, half, src=src)

    def partner(self):
        for half in HALVES:
            there = self.slots.at[self.place.slot(0, 1), half]
            remote(
                there, there, self.sems[2].at[half], self.sems[3].at[half], ctx=self.place.partner
            ).wait_recv()
            for way in (0, 1):
                self.z_start(1, way, 1, half)

    def hop(self, chain, step, between=None):
        for half in HALVES:
            for way in (0, 1):
                if LEN[chain][way] < step:
                    continue
                if between is not None:
                    between()
                self.z_wait(chain, way, step, half)
                if step < LEN[chain][way]:
                    self.z_start(chain, way, step + 1, half)

    def finish(self):
        for copy in self.started:
            copy.wait_send()


GATHER_SEMS = [
    pltpu.SemaphoreType.DMA((2, 2, 4, 2)),
    pltpu.SemaphoreType.DMA((2, 2, 4, 2)),
    pltpu.SemaphoreType.DMA((2,)),
    pltpu.SemaphoreType.DMA((2,)),
]


def exchange_kernel(
    q_ref, k_ref, v_ref, nk_ref, nv_ref, slots_ref, counts_ref, w_ref,
    g_out, k_out, vt_out, new_out, slots_out, counts_out, w_out,
    v_buf, l_sem, c_send, c_recv, *sems,
):
    place = Place()
    pages = v_buf.shape[0]
    local = [
        pltpu.make_async_copy(src, dst, l_sem.at[i])
        for i, (src, dst) in enumerate(
            (
                (v_ref, v_buf),
                (k_ref, k_out.at[0]),
                (q_ref, g_out.at[place.slot(0, 0)]),
                (nk_ref, new_out.at[0, 0]),
                (nv_ref, new_out.at[0, 1]),
                (slots_ref, slots_out.at[0]),
                (counts_ref, counts_out.at[0]),
                (w_ref, w_out.at[0]),
            )
        )
    ]
    for copy in local:
        copy.start()
    greet([dict(ctx=where) for where in (place.above, place.below, place.partner, place.sibling)])

    gather = Gather(place, g_out, lambda half: q_ref.at[half], *sems)
    for half in HALVES:
        gather.start(half)

    to_sibling = []

    def give(src, dst):
        i = len(to_sibling)
        copy = remote(src, dst, c_send.at[i], c_recv.at[i], ctx=place.sibling)
        copy.start()
        to_sibling.append(copy)

    give(slots_ref, slots_out.at[1])
    give(counts_ref, counts_out.at[1])
    give(nk_ref, new_out.at[1, 0])
    give(nv_ref, new_out.at[1, 1])
    quarter = pages // 4
    for i in range(4):
        part = pl.ds(i * quarter, quarter)
        give(k_ref.at[part], k_out.at[1, part])
    give(w_ref, w_out.at[1])

    todo = list(range(16))
    each = pages // 16

    def between():
        if not todo:
            return
        i = todo.pop(0)
        if i == 0:
            local[0].wait()

        def turn(p, _):
            vt_out[0, p, 0:HEAD, :] = v_buf[p].T
            vt_out[0, p, HEAD:MSG, :] = jnp.ones((MSG - HEAD, PAGE), BF16)
            vt_out[1, p, HEAD:MSG, :] = jnp.ones((MSG - HEAD, PAGE), BF16)
            return 0

        lax.fori_loop(i * each, (i + 1) * each, turn, 0)
        if i % 4 == 3:
            part = pl.ds((i - 3) * each, 4 * each), pl.ds(0, HEAD)
            give(vt_out.at[(0,) + part], vt_out.at[(1,) + part])

    gather.hop(0, 1, between)
    gather.partner()
    gather.hop(0, 2, between)
    gather.hop(1, 1, between)
    gather.hop(0, 3, between)
    gather.hop(1, 2, between)
    while todo:
        between()
    gather.hop(0, 4)
    gather.hop(1, 3)
    gather.hop(1, 4)
    gather.finish()
    for copy in local[1:]:
        copy.wait()
    for copy in to_sibling:
        copy.wait()


def exchange(q, k, v, nk, nv, slots, counts, w):
    pages = v.shape[0]
    n_give = 13
    return pl.pallas_call(
        exchange_kernel,
        out_shape=(
            jax.ShapeDtypeStruct((COLUMN, 2, HALF, HEAD), BF16),
            jax.ShapeDtypeStruct((2, pages, PAGE, HEAD), BF16),
            jax.ShapeDtypeStruct((2, pages, MSG, PAGE), BF16),
            jax.ShapeDtypeStruct((2, 2, QTOK, HEAD), BF16),
            jax.ShapeDtypeStruct((2,) + slots.shape, jnp.int32),
            jax.ShapeDtypeStruct((2,) + counts.shape, jnp.int32),
            jax.ShapeDtypeStruct((2,) + w.shape, BF16),
        ),
        in_specs=[pl.BlockSpec(memory_space=pltpu.HBM)] * 8,
        out_specs=[pl.BlockSpec(memory_space=pltpu.VMEM)] * 7,
        scratch_shapes=[
            pltpu.VMEM((pages, PAGE, HEAD), BF16),
            pltpu.SemaphoreType.DMA((8,)),
            pltpu.SemaphoreType.DMA((n_give,)),
            pltpu.SemaphoreType.DMA((n_give,)),
        ]
        + GATHER_SEMS,
        compiler_params=pltpu.CompilerParams(
            collective_id=0, has_side_effects=True, vmem_limit_bytes=24 * MIB
        ),
        name="exchange",
    )(q, k, v, nk, nv, slots, counts, w)


def write_message(ref, top, total, sums):
    ref[0:HEAD, :] = sums.astype(BF16)
    high = total.astype(BF16).astype(F32)
    low = total - high
    row = lax.broadcasted_iota(jnp.int32, (MSG - HEAD, HALF), 0)
    stats = jnp.where(row == 0, top, jnp.where(row == 1, high, jnp.where(row == 2, low, 0.0)))
    ref[HEAD:MSG, :] = stats.astype(BF16)


def merged(refs):
    tops, totals = [], []
    for ref in refs:
        stats = ref[HEAD:MSG, :].astype(F32)
        tops.append(stats[0:1, :])
        totals.append(stats[1:2, :] + stats[2:3, :])
    top = tops[0]
    for other in tops[1:]:
        top = jnp.maximum(top, other)
    total = None
    sums = None
    for ref, t, n in zip(refs, tops, totals):
        scale = jnp.exp2(t - top)
        piece = ref[0:HEAD, :].astype(F32) * scale
        total = n * scale if total is None else total + n * scale
        sums = piece if sums is None else sums + piece
    return top, total, sums


def partial_kernel(slots_ref, counts_ref, q_ref, k_ref, vt_ref, new_ref, out_ref, nvt, earlier):
    me = lax.axis_index("ctx")
    core = me % 2
    pages = k_ref.shape[1]
    contract = (((1,), (1,)), ((), ()))
    fresh = 2 * QTOK
    rows = 2 * HALF
    nvt[0:HEAD, :] = new_ref[:, 1].reshape(fresh, HEAD).astype(F32).T.astype(BF16)
    nvt[HEAD:MSG, :] = jnp.ones((MSG - HEAD, fresh), BF16)

    def block_of(slot):
        return slot * 2 + core

    def attend(slot, n, start):
        b = block_of(slot)
        own = counts_ref[0, 0, b]
        live_pages = own + counts_ref[1, 0, b] - start
        q = q_ref[slot].reshape(rows, HEAD)
        new = lax.dot_general(new_ref[:, 0].reshape(fresh, HEAD), q, contract, preferred_element_type=F32)
        key = lax.broadcasted_iota(jnp.int32, (fresh, rows), 0)
        held = jnp.where(key < QTOK, me * QTOK, (me + 1 - 2 * core) * QTOK - QTOK)
        token = lax.broadcasted_iota(jnp.int32, (fresh, rows), 1) // GROUP
        live = key + held <= jnp.where(start == 0, token + b * QTOK, -1)
        new = jnp.where(live, new, NEG_FILL)
        top = jnp.max(new, axis=0, keepdims=True)
        scores, values = [], []
        for i in range(n):
            at = start + i
            mine = slots_ref[0, jnp.minimum(at, MOST - 1), b]
            theirs = slots_ref[1, jnp.clip(at - own, 0, MOST - 1), b]
            side = jnp.where(at < own, 0, 1)
            page = jnp.where(at < own, mine, theirs)
            score = lax.dot_general(k_ref[side, page], q, contract, preferred_element_type=F32)
            scores.append(score)
            values.append(vt_ref[side, page])
            most = jnp.max(score, axis=0, keepdims=True)
            top = jnp.maximum(top, jnp.where(i < live_pages, most, NEG_FILL))
        top = (top * FACTOR).astype(BF16).astype(F32)
        weights = jnp.where(live, jnp.exp2(new * FACTOR - top), 0.0).astype(BF16)
        both = jnp.dot(nvt[...], weights, preferred_element_type=F32)
        if n:
            weights = [
                jnp.exp2(s * FACTOR - jnp.where(i < live_pages, top, -NEG_FILL)).astype(BF16)
                for i, s in enumerate(scores)
            ]
            both = both + jnp.dot(
                jnp.concatenate(values, axis=1), jnp.concatenate(weights, axis=0), preferred_element_type=F32
            )
        return top, both

    def pair(i, _):
        slots = 2 * i, 2 * i + 1
        counts = [counts_ref[0, 0, block_of(s)] + counts_ref[1, 0, block_of(s)] for s in slots]
        most = jnp.maximum(counts[0], counts[1])

        def turn(r, _):
            start = r * MOST

            @pl.when(r > 0)
            def _():
                earlier[...] = out_ref[pl.ds(2 * i, 2)]

            steps = (jnp.minimum(most - start, MOST) + 1) // 2

            def case(n):
                def run():
                    for slot, (top, both) in [(s, attend(s, n, start)) for s in slots]:
                        for half in HALVES:
                            cols = slice(half * HALF, (half + 1) * HALF)
                            write_message(
                                out_ref.at[slot, half], top[:, cols], both[HEAD : HEAD + 1, cols], both[0:HEAD, cols]
                            )

                return run

            for n in range(0, MOST + 1, 2):
                pl.when(steps == n // 2)(case(n))

            @pl.when(r > 0)
            def _():
                for j, slot in enumerate(slots):
                    for half in HALVES:
                        whole = merged([out_ref.at[slot, half], earlier.at[j, half]])
                        write_message(out_ref.at[slot, half], *whole)

            return 0

        lax.fori_loop(0, jnp.where(most > MOST, 2, 1), turn, 0)
        return 0

    lax.fori_loop(0, COLUMN // 2, pair, 0)


def partials(slots, counts, q, k, vt, new):
    return pl.pallas_call(
        partial_kernel,
        out_shape=jax.ShapeDtypeStruct((COLUMN, 2, MSG, HALF), BF16),
        in_specs=[pl.BlockSpec(memory_space=pltpu.SMEM)] * 2 + [pl.BlockSpec(memory_space=pltpu.VMEM)] * 4,
        out_specs=pl.BlockSpec(memory_space=pltpu.VMEM),
        scratch_shapes=[pltpu.VMEM((MSG, 2 * QTOK), BF16), pltpu.VMEM((2, 2, MSG, HALF), BF16)],
        compiler_params=pltpu.CompilerParams(vmem_limit_bytes=24 * MIB),
        name="partials",
    )(slots, counts, q, k, vt, new)


def finish_kernel(
    p_ref, w_ref, out_ref,
    t_buf, r_buf, y_buf, turned, a_buf, mine_buf, kv_buf,
    rz_send, rz_recv, ry_send, ry_recv, kv_send, kv_recv, *sems,
):
    place = Place()
    peers = [dict(ctx=where) for where in (place.above, place.below, place.partner, place.sibling)]
    for off in range(1, ZS):
        other = lax.rem(place.kv + off, ZS)
        peers += [dict(kv=other), dict(ctx=place.sibling, kv=other)]
    greet(peers)
    started = []

    def begin(copy):
        copy.start()
        started.append(copy)

    def mine(dz, chain, half):
        return p_ref.at[place.slot(dz, chain), half]

    def z_copy(chain, way, step, half):
        at = chain, way, step - 1, half
        src = mine(WAYS[way] * LEN[chain][1 - way], chain, half) if step == 1 else t_buf.at[at]
        return remote(src, r_buf.at[at], rz_send.at[at], rz_recv.at[at], ctx=place.along(way))

    for step in range(1, 5):
        for chain in (1, 0):
            for half in HALVES:
                for way in (0, 1):
                    length = LEN[chain][1 - way]
                    if step > length:
                        continue
                    if step > 1:
                        z_copy(chain, way, step - 1, half).wait_recv()
                        parts = [
                            mine(WAYS[way] * (length + 1 - step), chain, half),
                            r_buf.at[chain, way, step - 2, half],
                        ]
                        write_message(t_buf.at[chain, way, step - 1, half], *merged(parts))
                    begin(z_copy(chain, way, step, half))

    def home(chain, half):
        parts = [mine(0, chain, half)]
        for way in (0, 1):
            length = LEN[chain][1 - way]
            z_copy(chain, way, length, half).wait_recv()
            parts.append(r_buf.at[chain, way, length - 1, half])
        return parts

    def y_copy(half):
        return remote(
            y_buf.at[0, half], y_buf.at[1, half], ry_send.at[half], ry_recv.at[half], ctx=place.partner
        )

    for half in HALVES:
        write_message(y_buf.at[0, half], *merged(home(1, half)))
        begin(y_copy(half))

    here = place.slot(0, 0)
    gather = Gather(place, a_buf, lambda half: a_buf.at[here, half], *sems)
    for half in HALVES:
        parts = home(0, half)
        y_copy(half).wait_recv()
        _, total, sums = merged(parts + [y_buf.at[1, half]])
        turned[half] = (sums * (1.0 / total)).T
        tokens = QTOK // 2
        for g in range(GROUP):
            a_buf[here, half, :, g * HEAD : (g + 1) * HEAD] = turned[
                half, pl.ds(g, tokens, stride=GROUP), :
            ].astype(BF16)
        gather.start(half)

    width = w_ref.shape[2]

    def project(dz):
        plane = lax.rem(place.z + dz + ZS, ZS)
        rows = a_buf[pl.ds(plane * 2, 2)].reshape(2 * QTOK, a_buf.shape[3])
        for side in (0, 1):
            done = jnp.dot(rows, w_ref[side], preferred_element_type=F32)
            mine_buf[plane, side] = done.astype(BF16)

        def copy(side, **where):
            return remote(
                mine_buf.at[plane, side], kv_buf.at[place.kv, side],
                kv_send.at[plane, side], kv_recv.at[place.kv, side], **where,
            )

        @pl.when(plane != place.kv)
        def _():
            copy(0, kv=plane).start()
            copy(1, ctx=place.sibling, kv=plane).start()

        @pl.when(plane == place.kv)
        def _():
            copy(1, ctx=place.sibling).start()

    gather.hop(0, 1)
    gather.partner()
    gather.hop(0, 2)
    project(0)
    gather.hop(1, 1)
    gather.hop(0, 3)
    project(1)
    project(-1)
    gather.hop(1, 2)
    gather.hop(0, 4)
    project(2)
    project(-2)
    gather.hop(1, 3)
    project(3)
    project(-3)
    gather.hop(1, 4)
    project(4)

    totals = [mine_buf[place.kv, 0].astype(F32), None]
    for off in range(ZS):
        other = lax.rem(place.kv + off, ZS)
        for side in (0, 1):
            if off == 0 and side == 0:
                continue
            where = dict(kv=other) if side == 0 else dict(ctx=place.sibling, kv=other)
            remote(
                mine_buf.at[other, side], kv_buf.at[other, side],
                kv_send.at[other, side], kv_recv.at[other, side], **where,
            ).wait()
            piece = kv_buf[other, side].astype(F32)
            totals[side] = piece if totals[side] is None else totals[side] + piece
    for side in (0, 1):
        core = place.core if side == 0 else 1 - place.core
        done = totals[side].astype(BF16).reshape(2, QTOK, width)
        for yh in (0, 1):
            out_ref[pl.ds(pl.multiple_of(yh * 2 * QTOK + core * QTOK, QTOK), QTOK), :] = done[yh]
    for copy in started:
        copy.wait_send()
    gather.finish()


def finish(p, w):
    depth, width = w.shape[1:]
    return pl.pallas_call(
        finish_kernel,
        out_shape=jax.ShapeDtypeStruct((4 * QTOK, width), BF16),
        in_specs=[pl.BlockSpec(memory_space=pltpu.VMEM)] * 2,
        out_specs=pl.BlockSpec(memory_space=pltpu.VMEM),
        scratch_shapes=[
            pltpu.VMEM((2, 2, 4, 2, MSG, HALF), BF16),
            pltpu.VMEM((2, 2, 4, 2, MSG, HALF), BF16),
            pltpu.VMEM((2, 2, MSG, HALF), BF16),
            pltpu.VMEM((2, HALF, HEAD), F32),
            pltpu.VMEM((COLUMN, 2, QTOK // 2, depth), BF16),
            pltpu.VMEM((ZS, 2, 2 * QTOK, width), BF16),
            pltpu.VMEM((ZS, 2, 2 * QTOK, width), BF16),
            pltpu.SemaphoreType.DMA((2, 2, 4, 2)),
            pltpu.SemaphoreType.DMA((2, 2, 4, 2)),
            pltpu.SemaphoreType.DMA((2,)),
            pltpu.SemaphoreType.DMA((2,)),
            pltpu.SemaphoreType.DMA((ZS, 2)),
            pltpu.SemaphoreType.DMA((ZS, 2)),
        ]
        + GATHER_SEMS,
        compiler_params=pltpu.CompilerParams(
            collective_id=1, has_side_effects=True, vmem_limit_bytes=24 * MIB
        ),
        name="finish",
    )(p, w)


def body(queries, new_keys, new_values, key_cache, value_cache, page_slots, page_counts, out_weight):
    q = queries.reshape(2, HALF, HEAD)
    nk = new_keys.reshape(QTOK, HEAD)
    nv = new_values.reshape(QTOK, HEAD)
    k = key_cache.reshape(-1, PAGE, HEAD)
    v = value_cache.reshape(-1, PAGE, HEAD)
    arrays = q, k, v, nk, nv, page_slots[0].T, page_counts, out_weight
    q_all, k_all, vt_all, new_all, slots, counts, w_all = exchange(
        *(pltpu.with_memory_space_constraint(array, pltpu.HBM) for array in arrays)
    )
    p = partials(slots, counts, q_all, k_all, vt_all, new_all)
    return finish(p, w_all)


def solution(mesh):
    placed = (
        P("ctx", "kv", None),
        P("ctx", "kv", None),
        P("ctx", "kv", None),
        P("ctx", "kv", None),
        P("ctx", "kv", None),
        P("ctx", None, None),
        P("ctx", None),
        P("kv", "ctx"),
    )
    return jax.shard_map(
        body, mesh=mesh, in_specs=placed, out_specs=P("kv", "ctx"), check_vma=False
    )
```

```python
import jax
import jax.numpy as jnp
from jax import lax
from jax.experimental import pallas as pl
from jax.experimental.pallas import tpu as pltpu
from jax.sharding import PartitionSpec as P

PAGE = 128
HEAD = 128
QTOK = 32
GROUP = 8
HALF = 128
MSG = 144
ZS = 8
COLUMN = 16
MOST = 8
TEAM = 4
NEG_FILL = -1e30
FACTOR = HEAD ** (-0.5) * 1.4426950408889634
MIB = 1 << 20
MESH = pl.DeviceIdType.MESH
BF16 = jnp.bfloat16
F32 = jnp.float32

WAYS = (1, -1)
HALVES = (0, 1)
FAR = 4


class Place:
    def __init__(self):
        self.me = lax.axis_index("ctx")
        self.kv = lax.axis_index("kv")
        self.z = self.me // 4
        self.yh = (self.me % 4) // 2
        self.core = self.me % 2
        self.partner = self.block(0, 1)
        self.sibling = self.z * 4 + self.yh * 2 + 1 - self.core
        self.first = jnp.where(self.z % 4 < 2, 1, 0)

    def neighbours(self):
        return [self.block(dz, chain) for chain in (0, 1) for dz in WAYS] + [self.partner, self.sibling]

    def slot(self, dz, chain):
        z = lax.rem(self.z + dz + ZS, ZS)
        return z * 2 + (1 - self.yh if chain else self.yh)

    def block(self, dz, chain):
        return self.slot(dz, chain) * 2 + self.core

    def ways(self):
        return self.first, 1 - self.first


def remote(src, dst, send, recv, **where):
    return pltpu.make_async_remote_copy(
        src_ref=src, dst_ref=dst, send_sem=send, recv_sem=recv, device_id=where, device_id_type=MESH
    )


def greet(wheres):
    barrier = pltpu.get_barrier_semaphore()
    for where in wheres:
        pl.semaphore_signal(barrier, inc=1, device_id=where, device_id_type=MESH)
    pl.semaphore_wait(barrier, len(wheres))


def sign(way):
    return 1 - 2 * way


class Gather:
    def __init__(self, place, slots, own, z_send, z_recv, y_send, y_recv):
        self.place, self.slots, self.own = place, slots, own
        self.z_send, self.z_recv, self.y_send, self.y_recv = z_send, z_recv, y_send, y_recv

    def hop_to(self, chain, way, step, half):
        at = chain, way, step - 1, half
        if step == 1:
            src, dst = self.own(half), self.slots.at[self.place.slot(0, 0), half]
        else:
            src = dst = self.slots.at[self.place.slot((1 - step) * sign(way), chain), half]
        target = self.place.block(sign(way), chain if step == 1 else 0)
        return remote(src, dst, self.z_send.at[at], self.z_recv.at[at], ctx=target)

    def hop_from(self, chain, way, step, half):
        at = chain, way, step - 1, half
        there = self.slots.at[self.place.slot(-step * sign(way), chain), half]
        return remote(there, there, self.z_send.at[at], self.z_recv.at[at], ctx=self.place.partner)

    def across(self, half):
        dst = self.slots.at[self.place.slot(0, 0), half]
        return remote(self.own(half), dst, self.y_send.at[half], self.y_recv.at[half], ctx=self.place.partner)

    def start(self, half):
        for chain in (0, 1):
            for way in (0, 1):
                self.hop_to(chain, way, 1, half).start()

    def start_across(self):
        for half in HALVES:
            self.across(half).start()

    def wait_across(self):
        for half in HALVES:
            there = self.slots.at[self.place.slot(0, 1), half]
            remote(
                there, there, self.y_send.at[half], self.y_recv.at[half], ctx=self.place.partner
            ).wait_recv()

    def hop(self, chain, step, between=None):
        for half in HALVES:
            if between is not None:
                between()
            if step == FAR:
                self.hop_from(chain, half, step, half).wait_recv()
                continue
            for way in self.place.ways():
                self.hop_from(chain, way, step, half).wait_recv()
                onward = self.hop_to(chain, way, step + 1, half)
                if step + 1 < FAR:
                    onward.start()
                else:
                    pl.when(way == half)(onward.start)

    def finish(self):
        for half in HALVES:
            self.across(half).wait_send()
            for chain in (0, 1):
                for step in range(1, FAR + 1):
                    for way in (0, 1) if step < FAR else (half,):
                        self.hop_to(chain, way, step, half).wait_send()


GATHER_SEMS = [
    pltpu.SemaphoreType.DMA((2, 2, 4, 2)),
    pltpu.SemaphoreType.DMA((2, 2, 4, 2)),
    pltpu.SemaphoreType.DMA((2,)),
    pltpu.SemaphoreType.DMA((2,)),
]


def exchange_kernel(
    q_ref, k_ref, v_ref, nk_ref, nv_ref, slots_ref, counts_ref, w_ref,
    g_out, k_out, vt_out, new_out, slots_out, counts_out, w_out,
    v_buf, l_sem, c_send, c_recv, *sems,
):
    place = Place()
    pages = v_buf.shape[0]
    local = [
        pltpu.make_async_copy(src, dst, l_sem.at[i])
        for i, (src, dst) in enumerate(
            (
                (v_ref, v_buf),
                (k_ref, k_out.at[0]),
                (q_ref, g_out.at[place.slot(0, 0)]),
                (nk_ref, new_out.at[0, 0]),
                (nv_ref, new_out.at[0, 1]),
                (slots_ref, slots_out.at[0]),
                (counts_ref, counts_out.at[0]),
                (w_ref, w_out.at[0]),
            )
        )
    ]
    for copy in local:
        copy.start()
    greet([dict(ctx=where) for where in place.neighbours()])

    gather = Gather(place, g_out, lambda half: q_ref.at[half], *sems)
    for half in HALVES:
        gather.start(half)
    gather.start_across()

    to_sibling = []

    def give(src, dst):
        i = len(to_sibling)
        copy = remote(src, dst, c_send.at[i], c_recv.at[i], ctx=place.sibling)
        copy.start()
        to_sibling.append(copy)

    give(slots_ref, slots_out.at[1])
    give(counts_ref, counts_out.at[1])
    give(nk_ref, new_out.at[1, 0])
    give(nv_ref, new_out.at[1, 1])
    quarter = pages // 4
    for i in range(4):
        part = pl.ds(i * quarter, quarter)
        give(k_ref.at[part], k_out.at[1, part])
    give(w_ref, w_out.at[1])

    todo = list(range(8))
    each = pages // 8

    def between():
        if not todo:
            return
        i = todo.pop(0)
        if i == 0:
            local[0].wait()

        def turn(p, _):
            vt_out[0, p, 0:HEAD, :] = v_buf[p].T
            vt_out[0, p, HEAD:MSG, :] = jnp.ones((MSG - HEAD, PAGE), BF16)
            vt_out[1, p, HEAD:MSG, :] = jnp.ones((MSG - HEAD, PAGE), BF16)
            return 0

        lax.fori_loop(i * each, (i + 1) * each, turn, 0)
        if i % 2 == 1:
            part = pl.ds((i - 1) * each, 2 * each), pl.ds(0, HEAD)
            give(vt_out.at[(0,) + part], vt_out.at[(1,) + part])

    for step in range(1, FAR):
        for chain in (0, 1):
            gather.hop(chain, step, between)
    while todo:
        between()
    for chain in (0, 1):
        gather.hop(chain, FAR)
    gather.wait_across()
    gather.finish()
    for copy in local[1:]:
        copy.wait()
    for copy in to_sibling:
        copy.wait()


def exchange(q, k, v, nk, nv, slots, counts, w):
    pages = v.shape[0]
    n_give = 13
    return pl.pallas_call(
        exchange_kernel,
        out_shape=(
            jax.ShapeDtypeStruct((COLUMN, 2, HALF, HEAD), BF16),
            jax.ShapeDtypeStruct((2, pages, PAGE, HEAD), BF16),
            jax.ShapeDtypeStruct((2, pages, MSG, PAGE), BF16),
            jax.ShapeDtypeStruct((2, 2, QTOK, HEAD), BF16),
            jax.ShapeDtypeStruct((2,) + slots.shape, jnp.int32),
            jax.ShapeDtypeStruct((2,) + counts.shape, jnp.int32),
            jax.ShapeDtypeStruct((2,) + w.shape, BF16),
        ),
        in_specs=[pl.BlockSpec(memory_space=pltpu.HBM)] * 8,
        out_specs=[pl.BlockSpec(memory_space=pltpu.VMEM)] * 7,
        scratch_shapes=[
            pltpu.VMEM((pages, PAGE, HEAD), BF16),
            pltpu.SemaphoreType.DMA((8,)),
            pltpu.SemaphoreType.DMA((n_give,)),
            pltpu.SemaphoreType.DMA((n_give,)),
        ]
        + GATHER_SEMS,
        compiler_params=pltpu.CompilerParams(
            collective_id=0, has_side_effects=True, vmem_limit_bytes=24 * MIB
        ),
        name="exchange",
    )(q, k, v, nk, nv, slots, counts, w)


def write_message(ref, top, total, sums):
    ref[0:HEAD, :] = sums.astype(BF16)
    high = total.astype(BF16).astype(F32)
    low = total - high
    row = lax.broadcasted_iota(jnp.int32, (MSG - HEAD, HALF), 0)
    stats = jnp.where(row == 0, top, jnp.where(row == 1, high, jnp.where(row == 2, low, 0.0)))
    ref[HEAD:MSG, :] = stats.astype(BF16)


def merged(refs):
    tops, totals = [], []
    for ref in refs:
        stats = ref[HEAD:MSG, :].astype(F32)
        tops.append(stats[0:1, :])
        totals.append(stats[1:2, :] + stats[2:3, :])
    top = tops[0]
    for other in tops[1:]:
        top = jnp.maximum(top, other)
    total = None
    sums = None
    for ref, t, n in zip(refs, tops, totals):
        scale = jnp.exp2(t - top)
        piece = ref[0:HEAD, :].astype(F32) * scale
        total = n * scale if total is None else total + n * scale
        sums = piece if sums is None else sums + piece
    return top, total, sums


def partial_kernel(
    slots_ref, counts_ref, q_ref, k_ref, vt_ref, new_ref, out_ref, nvt, lag, earlier, count_of, order
):
    me = lax.axis_index("ctx")
    core = me % 2
    contract = (((1,), (1,)), ((), ()))
    fresh = 2 * QTOK
    rows = 2 * HALF
    nvt[0:HEAD, :] = new_ref[:, 1].reshape(fresh, HEAD).astype(F32).T.astype(BF16)
    nvt[HEAD:MSG, :] = jnp.ones((MSG - HEAD, fresh), BF16)
    key = lax.broadcasted_iota(jnp.int32, (fresh, rows), 0)
    held = jnp.where(key < QTOK, me * QTOK, (me - 2 * core) * QTOK)
    lag[...] = key + held - lax.broadcasted_iota(jnp.int32, (fresh, rows), 1) // GROUP

    counts = [counts_ref[0, 0, 2 * j + core] + counts_ref[1, 0, 2 * j + core] for j in range(COLUMN)]
    for j in range(COLUMN):
        rank = 0
        for i in range(COLUMN):
            if i != j:
                ahead = counts[i] >= counts[j] if i < j else counts[i] > counts[j]
                rank = rank + ahead.astype(jnp.int32)
        order[rank] = j
        count_of[j] = counts[j]

    def attend(slot, n, start):
        b = slot * 2 + core
        own = counts_ref[0, 0, b]
        live_pages = count_of[slot] - start
        q = q_ref[slot].reshape(rows, HEAD)
        new = lax.dot_general(new_ref[:, 0].reshape(fresh, HEAD), q, contract, preferred_element_type=F32)
        live = lag[...] <= jnp.where(start == 0, b * QTOK, -2 * COLUMN * QTOK)
        new = jnp.where(live, new, NEG_FILL)
        top = jnp.max(new, axis=0, keepdims=True)
        scores, values = [], []
        for i in range(n):
            at = start + i
            mine = slots_ref[0, jnp.minimum(at, MOST - 1), b]
            theirs = slots_ref[1, jnp.clip(at - own, 0, MOST - 1), b]
            side = jnp.where(at < own, 0, 1)
            page = jnp.where(at < own, mine, theirs)
            score = lax.dot_general(k_ref[side, page], q, contract, preferred_element_type=F32)
            scores.append(score)
            values.append(vt_ref[side, page])
            most = jnp.max(score, axis=0, keepdims=True)
            top = jnp.maximum(top, jnp.where(i < live_pages, most, NEG_FILL))
        top = (top * FACTOR).astype(BF16).astype(F32)
        weights = jnp.where(live, jnp.exp2(new * FACTOR - top), 0.0).astype(BF16)
        both = jnp.dot(nvt[...], weights, preferred_element_type=F32)
        if n:
            weights = [
                jnp.exp2(s * FACTOR - jnp.where(i < live_pages, top, -NEG_FILL)).astype(BF16)
                for i, s in enumerate(scores)
            ]
            both = both + jnp.dot(
                jnp.concatenate(values, axis=1), jnp.concatenate(weights, axis=0), preferred_element_type=F32
            )
        return top, both

    def team(i, _):
        slots = [order[i * TEAM + j] for j in range(TEAM)]
        most = count_of[slots[0]]

        def turn(r, _):
            start = r * MOST

            @pl.when(r > 0)
            def _():
                for j, slot in enumerate(slots):
                    earlier[j] = out_ref[slot]

            steps = (jnp.minimum(most - start, MOST) + 1) // 2

            def case(n):
                def run():
                    for slot, (top, both) in [(s, attend(s, n, start)) for s in slots]:
                        for half in HALVES:
                            cols = slice(half * HALF, (half + 1) * HALF)
                            write_message(
                                out_ref.at[slot, half], top[:, cols], both[HEAD : HEAD + 1, cols], both[0:HEAD, cols]
                            )

                return run

            for n in range(0, MOST + 1, 2):
                pl.when(steps == n // 2)(case(n))

            @pl.when(r > 0)
            def _():
                for j, slot in enumerate(slots):
                    for half in HALVES:
                        whole = merged([out_ref.at[slot, half], earlier.at[j, half]])
                        write_message(out_ref.at[slot, half], *whole)

            return 0

        lax.fori_loop(0, jnp.where(most > MOST, 2, 1), turn, 0)
        return 0

    lax.fori_loop(0, COLUMN // TEAM, team, 0)


def partials(slots, counts, q, k, vt, new):
    return pl.pallas_call(
        partial_kernel,
        out_shape=jax.ShapeDtypeStruct((COLUMN, 2, MSG, HALF), BF16),
        in_specs=[pl.BlockSpec(memory_space=pltpu.SMEM)] * 2 + [pl.BlockSpec(memory_space=pltpu.VMEM)] * 4,
        out_specs=pl.BlockSpec(memory_space=pltpu.VMEM),
        scratch_shapes=[
            pltpu.VMEM((MSG, 2 * QTOK), BF16),
            pltpu.VMEM((2 * QTOK, 2 * HALF), jnp.int32),
            pltpu.VMEM((TEAM, 2, MSG, HALF), BF16),
            pltpu.SMEM((COLUMN,), jnp.int32),
            pltpu.SMEM((COLUMN,), jnp.int32),
        ],
        compiler_params=pltpu.CompilerParams(vmem_limit_bytes=24 * MIB),
        name="partials",
    )(slots, counts, q, k, vt, new)


def finish_kernel(
    p_ref, w_ref, out_ref,
    t_buf, r_buf, y_buf, turned, a_buf, mine_buf, kv_buf,
    rz_send, rz_recv, ry_send, ry_recv, kv_send, kv_recv, *sems,
):
    place = Place()
    peers = [dict(ctx=where) for where in place.neighbours()]
    for off in range(1, ZS):
        other = lax.rem(place.kv + off, ZS)
        peers += [dict(kv=other), dict(ctx=place.sibling, kv=other)]
    greet(peers)

    def mine(dz, chain, half):
        return p_ref.at[place.slot(dz, chain), half]

    def fold_to(chain, way, left, half):
        at = chain, way, left - 1, half
        entry = left == FAR or (left == FAR - 1 and isinstance(way, int) and way != half)
        src = mine(sign(way) * left, chain, half) if entry else t_buf.at[at]
        target = place.block(sign(way), chain if left == 1 else 0)
        return remote(src, r_buf.at[at], rz_send.at[at], rz_recv.at[at], ctx=target)

    def fold_from(chain, way, left, half):
        at = chain, way, left - 1, half
        remote(r_buf.at[at], r_buf.at[at], rz_send.at[at], rz_recv.at[at], ctx=place.partner).wait_recv()
        return r_buf.at[at]

    def fold(chain, way, left, half):
        parts = [mine(sign(way) * left, chain, half), fold_from(chain, way, left + 1, half)]
        write_message(t_buf.at[chain, way, left - 1, half], *merged(parts))
        fold_to(chain, way, left, half).start()

    def y_copy(half):
        return remote(
            mine(0, 1, half), y_buf.at[half], ry_send.at[half], ry_recv.at[half], ctx=place.partner
        )

    for half in HALVES:
        for chain in (1, 0):
            fold_to(chain, half, FAR, half).start()
    for half in HALVES:
        for chain in (1, 0):
            fold_to(chain, 1 - half, FAR - 1, half).start()
    for half in HALVES:
        y_copy(half).start()
    for half in HALVES:
        for chain in (1, 0):
            fold(chain, half, FAR - 1, half)
    for left in (2, 1):
        for half in HALVES:
            for chain in (1, 0):
                for way in place.ways():
                    fold(chain, way, left, half)

    here = place.slot(0, 0)
    gather = Gather(place, a_buf, lambda half: a_buf.at[here, half], *sems)
    for half in HALVES:
        parts = [mine(0, 0, half)]
        for chain in (1, 0):
            for way in (0, 1):
                parts.append(fold_from(chain, way, 1, half))
        remote(y_buf.at[half], y_buf.at[half], ry_send.at[half], ry_recv.at[half], ctx=place.partner).wait_recv()
        _, total, sums = merged(parts + [y_buf.at[half]])
        turned[half] = (sums * (1.0 / total)).T
        tokens = QTOK // 2
        for g in range(GROUP):
            a_buf[here, half, :, g * HEAD : (g + 1) * HEAD] = turned[
                half, pl.ds(g, tokens, stride=GROUP), :
            ].astype(BF16)
        gather.start(half)
    gather.start_across()

    width = w_ref.shape[2]

    def project(dz):
        plane = lax.rem(place.z + dz + ZS, ZS)
        rows = a_buf[pl.ds(plane * 2, 2)].reshape(2 * QTOK, a_buf.shape[3])
        for side in (0, 1):
            done = jnp.dot(rows, w_ref[side], preferred_element_type=F32)
            mine_buf[plane, side] = done.astype(BF16)

        def copy(side, **where):
            return remote(
                mine_buf.at[plane, side], kv_buf.at[place.kv, side],
                kv_send.at[plane, side], kv_recv.at[place.kv, side], **where,
            )

        @pl.when(plane != place.kv)
        def _():
            copy(0, kv=plane).start()
            copy(1, ctx=place.sibling, kv=plane).start()

        @pl.when(plane == place.kv)
        def _():
            copy(1, ctx=place.sibling).start()

    for step in range(1, FAR):
        for chain in (0, 1):
            gather.hop(chain, step)
        if step == 1:
            gather.wait_across()
            project(0)
        else:
            project(step - 1)
            project(1 - step)
    project(FAR - 1)
    project(1 - FAR)
    for chain in (0, 1):
        gather.hop(chain, FAR)
    project(FAR)

    totals = [mine_buf[place.kv, 0].astype(F32), None]
    for off in range(ZS):
        other = lax.rem(place.kv + off, ZS)
        for side in (0, 1):
            if off == 0 and side == 0:
                continue
            where = dict(kv=other) if side == 0 else dict(ctx=place.sibling, kv=other)
            remote(
                mine_buf.at[other, side], kv_buf.at[other, side],
                kv_send.at[other, side], kv_recv.at[other, side], **where,
            ).wait()
            piece = kv_buf[other, side].astype(F32)
            totals[side] = piece if totals[side] is None else totals[side] + piece
    for side in (0, 1):
        core = place.core if side == 0 else 1 - place.core
        done = totals[side].astype(BF16).reshape(2, QTOK, width)
        for yh in (0, 1):
            out_ref[pl.ds(pl.multiple_of(yh * 2 * QTOK + core * QTOK, QTOK), QTOK), :] = done[yh]
    for half in HALVES:
        y_copy(half).wait_send()
        for chain in (0, 1):
            for left in range(1, FAR + 1):
                for way in (0, 1) if left < FAR else (half,):
                    fold_to(chain, way, left, half).wait_send()
    gather.finish()


def finish(p, w):
    depth, width = w.shape[1:]
    return pl.pallas_call(
        finish_kernel,
        out_shape=jax.ShapeDtypeStruct((4 * QTOK, width), BF16),
        in_specs=[pl.BlockSpec(memory_space=pltpu.VMEM)] * 2,
        out_specs=pl.BlockSpec(memory_space=pltpu.VMEM),
        scratch_shapes=[
            pltpu.VMEM((2, 2, 4, 2, MSG, HALF), BF16),
            pltpu.VMEM((2, 2, 4, 2, MSG, HALF), BF16),
            pltpu.VMEM((2, MSG, HALF), BF16),
            pltpu.VMEM((2, HALF, HEAD), F32),
            pltpu.VMEM((COLUMN, 2, QTOK // 2, depth), BF16),
            pltpu.VMEM((ZS, 2, 2 * QTOK, width), BF16),
            pltpu.VMEM((ZS, 2, 2 * QTOK, width), BF16),
            pltpu.SemaphoreType.DMA((2, 2, 4, 2)),
            pltpu.SemaphoreType.DMA((2, 2, 4, 2)),
            pltpu.SemaphoreType.DMA((2,)),
            pltpu.SemaphoreType.DMA((2,)),
            pltpu.SemaphoreType.DMA((ZS, 2)),
            pltpu.SemaphoreType.DMA((ZS, 2)),
        ]
        + GATHER_SEMS,
        compiler_params=pltpu.CompilerParams(
            collective_id=1, has_side_effects=True, vmem_limit_bytes=24 * MIB
        ),
        name="finish",
    )(p, w)


def body(queries, new_keys, new_values, key_cache, value_cache, page_slots, page_counts, out_weight):
    q = queries.reshape(2, HALF, HEAD)
    nk = new_keys.reshape(QTOK, HEAD)
    nv = new_values.reshape(QTOK, HEAD)
    k = key_cache.reshape(-1, PAGE, HEAD)
    v = value_cache.reshape(-1, PAGE, HEAD)
    arrays = q, k, v, nk, nv, page_slots[0].T, page_counts, out_weight
    q_all, k_all, vt_all, new_all, slots, counts, w_all = exchange(
        *(pltpu.with_memory_space_constraint(array, pltpu.HBM) for array in arrays)
    )
    p = partials(slots, counts, q_all, k_all, vt_all, new_all)
    return finish(p, w_all)


def solution(mesh):
    placed = (
        P("ctx", "kv", None),
        P("ctx", "kv", None),
        P("ctx", "kv", None),
        P("ctx", "kv", None),
        P("ctx", "kv", None),
        P("ctx", None, None),
        P("ctx", None),
        P("kv", "ctx"),
    )
    return jax.shard_map(
        body, mesh=mesh, in_specs=placed, out_specs=P("kv", "ctx"), check_vma=False
    )
```

```python
import jax
import jax.numpy as jnp
from jax import lax
from jax.experimental import pallas as pl
from jax.experimental.pallas import tpu as pltpu
from jax.sharding import PartitionSpec as P

PAGE = 128
HEAD = 128
QTOK = 32
GROUP = 8
HALF = 128
MSG = 144
ZS = 8
COLUMN = 16
MOST = 8
TEAM = 4
NEG_FILL = -1e30
FACTOR = HEAD ** (-0.5) * 1.4426950408889634
MIB = 1 << 20
MESH = pl.DeviceIdType.MESH
BF16 = jnp.bfloat16
F32 = jnp.float32

WAYS = (1, -1)
HALVES = (0, 1)
FAR = 4
Q_PIECES = 2


class Place:
    def __init__(self):
        self.me = lax.axis_index("ctx")
        self.kv = lax.axis_index("kv")
        self.z = self.me // 4
        self.yh = (self.me % 4) // 2
        self.core = self.me % 2
        self.partner = self.block(0, 1)
        self.sibling = self.z * 4 + self.yh * 2 + 1 - self.core
        self.first = jnp.where(self.z % 4 < 2, 1, 0)

    def neighbours(self):
        near = [self.block(dz, chain) for chain in (0, 1) for dz in WAYS]
        return near + [self.block(2 * dz, 0) for dz in WAYS] + [self.partner, self.sibling]

    def slot(self, dz, chain):
        z = lax.rem(self.z + dz + ZS, ZS)
        return z * 2 + (1 - self.yh if chain else self.yh)

    def block(self, dz, chain):
        return self.slot(dz, chain) * 2 + self.core

    def ways(self):
        return self.first, 1 - self.first


def remote(src, dst, send, recv, **where):
    return pltpu.make_async_remote_copy(
        src_ref=src, dst_ref=dst, send_sem=send, recv_sem=recv, device_id=where, device_id_type=MESH
    )


def greet(wheres):
    barrier = pltpu.get_barrier_semaphore()
    for where in wheres:
        pl.semaphore_signal(barrier, inc=1, device_id=where, device_id_type=MESH)
    pl.semaphore_wait(barrier, len(wheres))


def sign(way):
    return 1 - 2 * way


class Gather:
    def __init__(self, place, slots, own, leap, z_send, z_recv, y_send, y_recv):
        self.place, self.slots, self.own, self.leap = place, slots, own, leap
        self.z_send, self.z_recv, self.y_send, self.y_recv = z_send, z_recv, y_send, y_recv
        self.pieces = range(slots.shape[1])

    def hop_to(self, chain, way, step, piece):
        at = chain, way, step - 1, piece
        jump = 2 if step == FAR and self.leap else 1
        if step == 1:
            src, dst = self.own(piece), self.slots.at[self.place.slot(0, 0), piece]
        else:
            src = dst = self.slots.at[self.place.slot((jump - step) * sign(way), chain), piece]
        target = self.place.block(jump * sign(way), chain if step == 1 else 0)
        return remote(src, dst, self.z_send.at[at], self.z_recv.at[at], ctx=target)

    def hop_from(self, chain, way, step, piece):
        at = chain, way, step - 1, piece
        there = self.slots.at[self.place.slot(-step * sign(way), chain), piece]
        return remote(there, there, self.z_send.at[at], self.z_recv.at[at], ctx=self.place.partner)

    def across(self, piece):
        dst = self.slots.at[self.place.slot(0, 0), piece]
        return remote(self.own(piece), dst, self.y_send.at[piece], self.y_recv.at[piece], ctx=self.place.partner)

    def start(self, piece):
        for chain in (0, 1):
            for way in (0, 1):
                self.hop_to(chain, way, 1, piece).start()

    def start_across(self):
        for piece in self.pieces:
            self.across(piece).start()

    def wait_across(self):
        for piece in self.pieces:
            there = self.slots.at[self.place.slot(0, 1), piece]
            remote(
                there, there, self.y_send.at[piece], self.y_recv.at[piece], ctx=self.place.partner
            ).wait_recv()

    def hop(self, chain, step, between=None):
        for piece in self.pieces:
            far = piece % 2
            if between is not None:
                between()
            if step == FAR:
                self.hop_from(chain, far, step, piece).wait_recv()
                continue
            for way in self.place.ways():
                self.hop_from(chain, way, step, piece).wait_recv()
                if step == FAR - (2 if self.leap else 1):
                    pl.when(way == far)(self.hop_to(chain, way, FAR, piece).start)
                if step < FAR - 1:
                    self.hop_to(chain, way, step + 1, piece).start()

    def finish(self):
        for piece in self.pieces:
            self.across(piece).wait_send()
            for chain in (0, 1):
                for step in range(1, FAR + 1):
                    for way in (0, 1) if step < FAR else (piece % 2,):
                        self.hop_to(chain, way, step, piece).wait_send()


def gather_sems(pieces):
    return [
        pltpu.SemaphoreType.DMA((2, 2, FAR, pieces)),
        pltpu.SemaphoreType.DMA((2, 2, FAR, pieces)),
        pltpu.SemaphoreType.DMA((pieces,)),
        pltpu.SemaphoreType.DMA((pieces,)),
    ]


def exchange_kernel(
    q_ref, k_ref, v_ref, nk_ref, nv_ref, slots_ref, counts_ref, w_ref,
    g_out, k_out, vt_out, new_out, slots_out, counts_out, w_out,
    v_buf, l_sem, c_send, c_recv, *sems,
):
    place = Place()
    pages = v_buf.shape[0]
    local = [
        pltpu.make_async_copy(src, dst, l_sem.at[i])
        for i, (src, dst) in enumerate(
            (
                (v_ref, v_buf),
                (k_ref, k_out.at[0]),
                (q_ref, g_out.at[place.slot(0, 0)]),
                (nk_ref, new_out.at[0, 0]),
                (nv_ref, new_out.at[0, 1]),
                (slots_ref, slots_out.at[0]),
                (counts_ref, counts_out.at[0]),
                (w_ref, w_out.at[0]),
            )
        )
    ]
    for copy in local:
        copy.start()
    greet([dict(ctx=where) for where in place.neighbours()])

    gather = Gather(place, g_out, lambda piece: q_ref.at[piece], True, *sems)
    for piece in gather.pieces:
        gather.start(piece)
    gather.start_across()

    to_sibling = []

    def give(src, dst):
        i = len(to_sibling)
        copy = remote(src, dst, c_send.at[i], c_recv.at[i], ctx=place.sibling)
        copy.start()
        to_sibling.append(copy)

    give(slots_ref, slots_out.at[1])
    give(counts_ref, counts_out.at[1])
    give(nk_ref, new_out.at[1, 0])
    give(nv_ref, new_out.at[1, 1])
    quarter = pages // 4
    for i in range(4):
        part = pl.ds(i * quarter, quarter)
        give(k_ref.at[part], k_out.at[1, part])
    give(w_ref, w_out.at[1])

    todo = list(range(16))
    each = pages // 16

    def between():
        if not todo:
            return
        i = todo.pop(0)
        if i == 0:
            local[0].wait()

        def turn(p, _):
            vt_out[0, p, 0:HEAD, :] = v_buf[p].T
            vt_out[0, p, HEAD:MSG, :] = jnp.ones((MSG - HEAD, PAGE), BF16)
            vt_out[1, p, HEAD:MSG, :] = jnp.ones((MSG - HEAD, PAGE), BF16)
            return 0

        lax.fori_loop(i * each, (i + 1) * each, turn, 0)
        if i % 4 == 3:
            part = pl.ds((i - 3) * each, 4 * each), pl.ds(0, HEAD)
            give(vt_out.at[(0,) + part], vt_out.at[(1,) + part])

    for _ in range(8):
        between()
    for step in range(1, FAR):
        for chain in (0, 1):
            gather.hop(chain, step, between)
    while todo:
        between()
    for chain in (0, 1):
        gather.hop(chain, FAR)
    gather.wait_across()
    gather.finish()
    for copy in local[1:]:
        copy.wait()
    for copy in to_sibling:
        copy.wait()


def exchange(q, k, v, nk, nv, slots, counts, w):
    pages = v.shape[0]
    n_give = 13
    return pl.pallas_call(
        exchange_kernel,
        out_shape=(
            jax.ShapeDtypeStruct((COLUMN,) + q.shape, BF16),
            jax.ShapeDtypeStruct((2, pages, PAGE, HEAD), BF16),
            jax.ShapeDtypeStruct((2, pages, MSG, PAGE), BF16),
            jax.ShapeDtypeStruct((2, 2, QTOK, HEAD), BF16),
            jax.ShapeDtypeStruct((2,) + slots.shape, jnp.int32),
            jax.ShapeDtypeStruct((2,) + counts.shape, jnp.int32),
            jax.ShapeDtypeStruct((2,) + w.shape, BF16),
        ),
        in_specs=[pl.BlockSpec(memory_space=pltpu.HBM)] * 8,
        out_specs=[pl.BlockSpec(memory_space=pltpu.VMEM)] * 7,
        scratch_shapes=[
            pltpu.VMEM((pages, PAGE, HEAD), BF16),
            pltpu.SemaphoreType.DMA((8,)),
            pltpu.SemaphoreType.DMA((n_give,)),
            pltpu.SemaphoreType.DMA((n_give,)),
        ]
        + gather_sems(q.shape[0]),
        compiler_params=pltpu.CompilerParams(
            collective_id=0, has_side_effects=True, vmem_limit_bytes=24 * MIB
        ),
        name="exchange",
    )(q, k, v, nk, nv, slots, counts, w)


def write_message(ref, top, total, sums):
    ref[0:HEAD, :] = sums.astype(BF16)
    high = total.astype(BF16).astype(F32)
    low = total - high
    row = lax.broadcasted_iota(jnp.int32, (MSG - HEAD, HALF), 0)
    stats = jnp.where(row == 0, top, jnp.where(row == 1, high, jnp.where(row == 2, low, 0.0)))
    ref[HEAD:MSG, :] = stats.astype(BF16)


def merged(refs):
    tops, totals = [], []
    for ref in refs:
        stats = ref[HEAD:MSG, :].astype(F32)
        tops.append(stats[0:1, :])
        totals.append(stats[1:2, :] + stats[2:3, :])
    top = tops[0]
    for other in tops[1:]:
        top = jnp.maximum(top, other)
    total = None
    sums = None
    for ref, t, n in zip(refs, tops, totals):
        scale = jnp.exp2(t - top)
        piece = ref[0:HEAD, :].astype(F32) * scale
        total = n * scale if total is None else total + n * scale
        sums = piece if sums is None else sums + piece
    return top, total, sums


def partial_kernel(
    slots_ref, counts_ref, q_ref, k_ref, vt_ref, new_ref, out_ref, nvt, lag, earlier, count_of, order
):
    me = lax.axis_index("ctx")
    core = me % 2
    contract = (((1,), (1,)), ((), ()))
    fresh = 2 * QTOK
    rows = 2 * HALF
    nvt[0:HEAD, :] = new_ref[:, 1].reshape(fresh, HEAD).astype(F32).T.astype(BF16)
    nvt[HEAD:MSG, :] = jnp.ones((MSG - HEAD, fresh), BF16)
    key = lax.broadcasted_iota(jnp.int32, (fresh, rows), 0)
    held = jnp.where(key < QTOK, me * QTOK, (me - 2 * core) * QTOK)
    lag[...] = key + held - lax.broadcasted_iota(jnp.int32, (fresh, rows), 1) // GROUP

    counts = [counts_ref[0, 0, 2 * j + core] + counts_ref[1, 0, 2 * j + core] for j in range(COLUMN)]
    for j in range(COLUMN):
        rank = 0
        for i in range(COLUMN):
            if i != j:
                ahead = counts[i] >= counts[j] if i < j else counts[i] > counts[j]
                rank = rank + ahead.astype(jnp.int32)
        order[rank] = j
        count_of[j] = counts[j]

    def attend(slot, n, start):
        b = slot * 2 + core
        own = counts_ref[0, 0, b]
        live_pages = count_of[slot] - start
        q = q_ref[slot].reshape(rows, HEAD)
        new = lax.dot_general(new_ref[:, 0].reshape(fresh, HEAD), q, contract, preferred_element_type=F32)
        live = lag[...] <= jnp.where(start == 0, b * QTOK, -2 * COLUMN * QTOK)
        new = jnp.where(live, new, NEG_FILL)
        top = jnp.max(new, axis=0, keepdims=True)
        scores, values = [], []
        for i in range(n):
            at = start + i
            mine = slots_ref[0, jnp.minimum(at, MOST - 1), b]
            theirs = slots_ref[1, jnp.clip(at - own, 0, MOST - 1), b]
            side = jnp.where(at < own, 0, 1)
            page = jnp.where(at < own, mine, theirs)
            score = lax.dot_general(k_ref[side, page], q, contract, preferred_element_type=F32)
            scores.append(score)
            values.append(vt_ref[side, page])
            most = jnp.max(score, axis=0, keepdims=True)
            top = jnp.maximum(top, jnp.where(i < live_pages, most, NEG_FILL))
        top = (top * FACTOR).astype(BF16).astype(F32)
        weights = jnp.where(live, jnp.exp2(new * FACTOR - top), 0.0).astype(BF16)
        both = jnp.dot(nvt[...], weights, preferred_element_type=F32)
        if n:
            weights = [
                jnp.exp2(s * FACTOR - jnp.where(i < live_pages, top, -NEG_FILL)).astype(BF16)
                for i, s in enumerate(scores)
            ]
            both = both + jnp.dot(
                jnp.concatenate(values, axis=1), jnp.concatenate(weights, axis=0), preferred_element_type=F32
            )
        return top, both

    def team(i, _):
        slots = [order[i * TEAM + j] for j in range(TEAM)]
        most = count_of[slots[0]]

        def turn(r, _):
            start = r * MOST

            @pl.when(r > 0)
            def _():
                for j, slot in enumerate(slots):
                    earlier[j] = out_ref[slot]

            steps = (jnp.minimum(most - start, MOST) + 1) // 2

            def case(n):
                def run():
                    for slot, (top, both) in [(s, attend(s, n, start)) for s in slots]:
                        for half in HALVES:
                            cols = slice(half * HALF, (half + 1) * HALF)
                            write_message(
                                out_ref.at[slot, half], top[:, cols], both[HEAD : HEAD + 1, cols], both[0:HEAD, cols]
                            )

                return run

            for n in range(0, MOST + 1, 2):
                pl.when(steps == n // 2)(case(n))

            @pl.when(r > 0)
            def _():
                for j, slot in enumerate(slots):
                    for half in HALVES:
                        whole = merged([out_ref.at[slot, half], earlier.at[j, half]])
                        write_message(out_ref.at[slot, half], *whole)

            return 0

        lax.fori_loop(0, jnp.where(most > MOST, 2, 1), turn, 0)
        return 0

    lax.fori_loop(0, COLUMN // TEAM, team, 0)


def partials(slots, counts, q, k, vt, new):
    return pl.pallas_call(
        partial_kernel,
        out_shape=jax.ShapeDtypeStruct((COLUMN, 2, MSG, HALF), BF16),
        in_specs=[pl.BlockSpec(memory_space=pltpu.SMEM)] * 2 + [pl.BlockSpec(memory_space=pltpu.VMEM)] * 4,
        out_specs=pl.BlockSpec(memory_space=pltpu.VMEM),
        scratch_shapes=[
            pltpu.VMEM((MSG, 2 * QTOK), BF16),
            pltpu.VMEM((2 * QTOK, 2 * HALF), jnp.int32),
            pltpu.VMEM((TEAM, 2, MSG, HALF), BF16),
            pltpu.SMEM((COLUMN,), jnp.int32),
            pltpu.SMEM((COLUMN,), jnp.int32),
        ],
        compiler_params=pltpu.CompilerParams(vmem_limit_bytes=24 * MIB),
        name="partials",
    )(slots, counts, q, k, vt, new)


def finish_kernel(
    p_ref, w_ref, out_ref,
    t_buf, r_buf, y_buf, turned, a_buf, mine_buf, kv_buf,
    rz_send, rz_recv, ry_send, ry_recv, kv_send, kv_recv, *sems,
):
    place = Place()
    peers = [dict(ctx=where) for where in place.neighbours()]
    for off in range(1, ZS):
        other = lax.rem(place.kv + off, ZS)
        peers += [dict(kv=other), dict(ctx=place.sibling, kv=other)]
    greet(peers)

    def mine(dz, chain, half):
        return p_ref.at[place.slot(dz, chain), half]

    def fold_to(chain, way, left, half):
        at = chain, way, left - 1, half
        entry = left == FAR or (left == FAR - 1 and isinstance(way, int) and way != half)
        src = mine(sign(way) * left, chain, half) if entry else t_buf.at[at]
        target = place.block(sign(way), chain if left == 1 else 0)
        return remote(src, r_buf.at[at], rz_send.at[at], rz_recv.at[at], ctx=target)

    def fold_from(chain, way, left, half):
        at = chain, way, left - 1, half
        remote(r_buf.at[at], r_buf.at[at], rz_send.at[at], rz_recv.at[at], ctx=place.partner).wait_recv()
        return r_buf.at[at]

    def fold(chain, way, left, half):
        parts = [mine(sign(way) * left, chain, half), fold_from(chain, way, left + 1, half)]
        write_message(t_buf.at[chain, way, left - 1, half], *merged(parts))
        fold_to(chain, way, left, half).start()

    def y_copy(half):
        return remote(
            mine(0, 1, half), y_buf.at[half], ry_send.at[half], ry_recv.at[half], ctx=place.partner
        )

    for half in HALVES:
        for chain in (1, 0):
            fold_to(chain, half, FAR, half).start()
    for half in HALVES:
        for chain in (1, 0):
            fold_to(chain, 1 - half, FAR - 1, half).start()
    for half in HALVES:
        y_copy(half).start()
    for half in HALVES:
        for chain in (1, 0):
            fold(chain, half, FAR - 1, half)
    for left in (2, 1):
        for half in HALVES:
            for chain in (1, 0):
                for way in place.ways():
                    fold(chain, way, left, half)

    here = place.slot(0, 0)
    gather = Gather(place, a_buf, lambda half: a_buf.at[here, half], False, *sems)
    for half in HALVES:
        parts = [mine(0, 0, half)]
        for chain in (1, 0):
            for way in (0, 1):
                parts.append(fold_from(chain, way, 1, half))
        remote(y_buf.at[half], y_buf.at[half], ry_send.at[half], ry_recv.at[half], ctx=place.partner).wait_recv()
        _, total, sums = merged(parts + [y_buf.at[half]])
        turned[half] = (sums * (1.0 / total)).T
        tokens = QTOK // 2
        for g in range(GROUP):
            a_buf[here, half, :, g * HEAD : (g + 1) * HEAD] = turned[
                half, pl.ds(g, tokens, stride=GROUP), :
            ].astype(BF16)
        gather.start(half)
    gather.start_across()

    width = w_ref.shape[2]

    def project(dz):
        plane = lax.rem(place.z + dz + ZS, ZS)
        rows = a_buf[pl.ds(plane * 2, 2)].reshape(2 * QTOK, a_buf.shape[3])
        for side in (0, 1):
            done = jnp.dot(rows, w_ref[side], preferred_element_type=F32)
            mine_buf[plane, side] = done.astype(BF16)

        def copy(side, **where):
            return remote(
                mine_buf.at[plane, side], kv_buf.at[place.kv, side],
                kv_send.at[plane, side], kv_recv.at[place.kv, side], **where,
            )

        @pl.when(plane != place.kv)
        def _():
            copy(0, kv=plane).start()
            copy(1, ctx=place.sibling, kv=plane).start()

        @pl.when(plane == place.kv)
        def _():
            copy(1, ctx=place.sibling).start()

    for step in range(1, FAR):
        for chain in (0, 1):
            gather.hop(chain, step)
        if step == 1:
            gather.wait_across()
            project(0)
        else:
            project(step - 1)
            project(1 - step)
    project(FAR - 1)
    project(1 - FAR)
    for chain in (0, 1):
        gather.hop(chain, FAR)
    project(FAR)

    totals = [mine_buf[place.kv, 0].astype(F32), None]
    for off in range(ZS):
        other = lax.rem(place.kv + off, ZS)
        for side in (0, 1):
            if off == 0 and side == 0:
                continue
            where = dict(kv=other) if side == 0 else dict(ctx=place.sibling, kv=other)
            remote(
                mine_buf.at[other, side], kv_buf.at[other, side],
                kv_send.at[other, side], kv_recv.at[other, side], **where,
            ).wait()
            piece = kv_buf[other, side].astype(F32)
            totals[side] = piece if totals[side] is None else totals[side] + piece
    for side in (0, 1):
        core = place.core if side == 0 else 1 - place.core
        done = totals[side].astype(BF16).reshape(2, QTOK, width)
        for yh in (0, 1):
            out_ref[pl.ds(pl.multiple_of(yh * 2 * QTOK + core * QTOK, QTOK), QTOK), :] = done[yh]
    for half in HALVES:
        y_copy(half).wait_send()
        for chain in (0, 1):
            for left in range(1, FAR + 1):
                for way in (0, 1) if left < FAR else (half,):
                    fold_to(chain, way, left, half).wait_send()
    gather.finish()


def finish(p, w):
    depth, width = w.shape[1:]
    return pl.pallas_call(
        finish_kernel,
        out_shape=jax.ShapeDtypeStruct((4 * QTOK, width), BF16),
        in_specs=[pl.BlockSpec(memory_space=pltpu.VMEM)] * 2,
        out_specs=pl.BlockSpec(memory_space=pltpu.VMEM),
        scratch_shapes=[
            pltpu.VMEM((2, 2, 4, 2, MSG, HALF), BF16),
            pltpu.VMEM((2, 2, 4, 2, MSG, HALF), BF16),
            pltpu.VMEM((2, MSG, HALF), BF16),
            pltpu.VMEM((2, HALF, HEAD), F32),
            pltpu.VMEM((COLUMN, 2, QTOK // 2, depth), BF16),
            pltpu.VMEM((ZS, 2, 2 * QTOK, width), BF16),
            pltpu.VMEM((ZS, 2, 2 * QTOK, width), BF16),
            pltpu.SemaphoreType.DMA((2, 2, 4, 2)),
            pltpu.SemaphoreType.DMA((2, 2, 4, 2)),
            pltpu.SemaphoreType.DMA((2,)),
            pltpu.SemaphoreType.DMA((2,)),
            pltpu.SemaphoreType.DMA((ZS, 2)),
            pltpu.SemaphoreType.DMA((ZS, 2)),
        ]
        + gather_sems(2),
        compiler_params=pltpu.CompilerParams(
            collective_id=1, has_side_effects=True, vmem_limit_bytes=24 * MIB
        ),
        name="finish",
    )(p, w)


def body(queries, new_keys, new_values, key_cache, value_cache, page_slots, page_counts, out_weight):
    q = queries.reshape(Q_PIECES, 2 * HALF // Q_PIECES, HEAD)
    nk = new_keys.reshape(QTOK, HEAD)
    nv = new_values.reshape(QTOK, HEAD)
    k = key_cache.reshape(-1, PAGE, HEAD)
    v = value_cache.reshape(-1, PAGE, HEAD)
    arrays = q, k, v, nk, nv, page_slots[0].T, page_counts, out_weight
    q_all, k_all, vt_all, new_all, slots, counts, w_all = exchange(
        *(pltpu.with_memory_space_constraint(array, pltpu.HBM) for array in arrays)
    )
    p = partials(slots, counts, q_all, k_all, vt_all, new_all)
    return finish(p, w_all)


def solution(mesh):
    placed = (
        P("ctx", "kv", None),
        P("ctx", "kv", None),
        P("ctx", "kv", None),
        P("ctx", "kv", None),
        P("ctx", "kv", None),
        P("ctx", None, None),
        P("ctx", None),
        P("kv", "ctx"),
    )
    return jax.shard_map(
        body, mesh=mesh, in_specs=placed, out_specs=P("kv", "ctx"), check_vma=False
    )
```

```python
import functools

import jax
import jax.numpy as jnp
from jax import lax
from jax.experimental import pallas as pl
from jax.experimental.pallas import tpu as pltpu
from jax.sharding import PartitionSpec as P

PAGE = 128
HEAD = 128
QTOK = 32
GROUP = 8
HALF = 128
MSG = 144
ZS = 8
COLUMN = 16
MOST = 8
TEAM = 4
NEG_FILL = -1e30
FACTOR = HEAD ** (-0.5) * 1.4426950408889634
MIB = 1 << 20
MESH = pl.DeviceIdType.MESH
BF16 = jnp.bfloat16
F32 = jnp.float32

WAYS = (1, -1)
HALVES = (0, 1)
FAR = 4
Q_PIECES = 2


class Place:
    def __init__(self):
        self.me = lax.axis_index("ctx")
        self.kv = lax.axis_index("kv")
        self.z = self.me // 4
        self.yh = (self.me % 4) // 2
        self.core = self.me % 2
        self.partner = self.block(0, 1)
        self.sibling = self.z * 4 + self.yh * 2 + 1 - self.core
        self.first = jnp.where(self.z % 4 < 2, 1, 0)

    def neighbours(self, jump):
        near = [self.block(dz, chain) for chain in (0, 1) for dz in WAYS]
        return near + [self.block(2 * dz, 0) for dz in WAYS if jump] + [self.partner, self.sibling]

    def slot(self, dz, chain):
        z = lax.rem(self.z + dz + ZS, ZS)
        return z * 2 + (1 - self.yh if chain else self.yh)

    def block(self, dz, chain):
        return self.slot(dz, chain) * 2 + self.core

    def ways(self):
        return self.first, 1 - self.first


def remote(src, dst, send, recv, **where):
    return pltpu.make_async_remote_copy(
        src_ref=src, dst_ref=dst, send_sem=send, recv_sem=recv, device_id=where, device_id_type=MESH
    )


def greet(wheres):
    barrier = pltpu.get_barrier_semaphore()
    for where in wheres:
        pl.semaphore_signal(barrier, inc=1, device_id=where, device_id_type=MESH)
    pl.semaphore_wait(barrier, len(wheres))


def sign(way):
    return 1 - 2 * way


class Gather:
    def __init__(self, place, slots, own, leap, z_send, z_recv, y_send, y_recv):
        self.place, self.slots, self.own, self.leap = place, slots, own, leap
        self.z_send, self.z_recv, self.y_send, self.y_recv = z_send, z_recv, y_send, y_recv
        self.pieces = range(slots.shape[1])

    def hop_to(self, chain, way, step, piece):
        at = chain, way, step - 1, piece
        jump = 2 if step == FAR and self.leap else 1
        if step == 1:
            src, dst = self.own(piece), self.slots.at[self.place.slot(0, 0), piece]
        else:
            src = dst = self.slots.at[self.place.slot((jump - step) * sign(way), chain), piece]
        target = self.place.block(jump * sign(way), chain if step == 1 else 0)
        return remote(src, dst, self.z_send.at[at], self.z_recv.at[at], ctx=target)

    def hop_from(self, chain, way, step, piece):
        at = chain, way, step - 1, piece
        there = self.slots.at[self.place.slot(-step * sign(way), chain), piece]
        return remote(there, there, self.z_send.at[at], self.z_recv.at[at], ctx=self.place.partner)

    def across(self, piece):
        dst = self.slots.at[self.place.slot(0, 0), piece]
        return remote(self.own(piece), dst, self.y_send.at[piece], self.y_recv.at[piece], ctx=self.place.partner)

    def start(self, piece):
        for chain in (0, 1):
            for way in (0, 1):
                self.hop_to(chain, way, 1, piece).start()

    def start_across(self):
        for piece in self.pieces:
            self.across(piece).start()

    def wait_across(self):
        for piece in self.pieces:
            there = self.slots.at[self.place.slot(0, 1), piece]
            remote(
                there, there, self.y_send.at[piece], self.y_recv.at[piece], ctx=self.place.partner
            ).wait_recv()

    def hop(self, chain, step, between=None):
        for piece in self.pieces:
            far = piece % 2
            if between is not None:
                between()
            if step == FAR:
                self.hop_from(chain, far, step, piece).wait_recv()
                continue
            for way in self.place.ways():
                self.hop_from(chain, way, step, piece).wait_recv()
                if step == FAR - (2 if self.leap else 1):
                    pl.when(way == far)(self.hop_to(chain, way, FAR, piece).start)
                if step < FAR - 1:
                    self.hop_to(chain, way, step + 1, piece).start()

    def finish(self):
        for piece in self.pieces:
            self.across(piece).wait_send()
            for chain in (0, 1):
                for step in range(1, FAR + 1):
                    for way in (0, 1) if step < FAR else (piece % 2,):
                        self.hop_to(chain, way, step, piece).wait_send()


def gather_sems(pieces):
    return [
        pltpu.SemaphoreType.DMA((2, 2, FAR, pieces)),
        pltpu.SemaphoreType.DMA((2, 2, FAR, pieces)),
        pltpu.SemaphoreType.DMA((pieces,)),
        pltpu.SemaphoreType.DMA((pieces,)),
    ]


def exchange_kernel(
    q_ref, k_ref, v_ref, nk_ref, nv_ref, slots_ref, counts_ref, w_ref,
    g_out, k_out, vt_out, new_out, slots_out, counts_out, w_out,
    v_buf, l_sem, c_send, c_recv, *sems,
):
    place = Place()
    pages = v_buf.shape[0]
    local = [
        pltpu.make_async_copy(src, dst, l_sem.at[i])
        for i, (src, dst) in enumerate(
            (
                (v_ref, v_buf),
                (k_ref, k_out.at[0]),
                (q_ref, g_out.at[place.slot(0, 0)]),
                (nk_ref, new_out.at[0, 0]),
                (nv_ref, new_out.at[0, 1]),
                (slots_ref, slots_out.at[0]),
                (counts_ref, counts_out.at[0]),
                (w_ref, w_out.at[0]),
            )
        )
    ]
    for copy in local:
        copy.start()
    greet([dict(ctx=where) for where in place.neighbours(True)])

    gather = Gather(place, g_out, lambda piece: q_ref.at[piece], True, *sems)
    for piece in gather.pieces:
        gather.start(piece)
    gather.start_across()

    to_sibling = []

    def give(src, dst):
        i = len(to_sibling)
        copy = remote(src, dst, c_send.at[i], c_recv.at[i], ctx=place.sibling)
        copy.start()
        to_sibling.append(copy)

    give(slots_ref, slots_out.at[1])
    give(counts_ref, counts_out.at[1])
    give(nk_ref, new_out.at[1, 0])
    give(nv_ref, new_out.at[1, 1])
    quarter = pages // 4
    for i in range(4):
        part = pl.ds(i * quarter, quarter)
        give(k_ref.at[part], k_out.at[1, part])
    give(w_ref, w_out.at[1])

    todo = list(range(16))
    each = pages // 16

    def between():
        if not todo:
            return
        i = todo.pop(0)
        if i == 0:
            local[0].wait()

        def turn(p, _):
            vt_out[0, p, 0:HEAD, :] = v_buf[p].T
            vt_out[0, p, HEAD:MSG, :] = jnp.ones((MSG - HEAD, PAGE), BF16)
            vt_out[1, p, HEAD:MSG, :] = jnp.ones((MSG - HEAD, PAGE), BF16)
            return 0

        lax.fori_loop(i * each, (i + 1) * each, turn, 0)
        if i % 4 == 3:
            part = pl.ds((i - 3) * each, 4 * each), pl.ds(0, HEAD)
            give(vt_out.at[(0,) + part], vt_out.at[(1,) + part])

    for _ in range(8):
        between()
    for step in range(1, FAR):
        for chain in (0, 1):
            gather.hop(chain, step, between)
    while todo:
        between()
    for chain in (0, 1):
        gather.hop(chain, FAR)
    gather.wait_across()
    gather.finish()
    for copy in local[1:]:
        copy.wait()
    for copy in to_sibling:
        copy.wait()


def exchange(q, k, v, nk, nv, slots, counts, w):
    pages = v.shape[0]
    n_give = 13
    return pl.pallas_call(
        exchange_kernel,
        out_shape=(
            jax.ShapeDtypeStruct((COLUMN,) + q.shape, BF16),
            jax.ShapeDtypeStruct((2, pages, PAGE, HEAD), BF16),
            jax.ShapeDtypeStruct((2, pages, MSG, PAGE), BF16),
            jax.ShapeDtypeStruct((2, 2, QTOK, HEAD), BF16),
            jax.ShapeDtypeStruct((2,) + slots.shape, jnp.int32),
            jax.ShapeDtypeStruct((2,) + counts.shape, jnp.int32),
            jax.ShapeDtypeStruct((2,) + w.shape, BF16),
        ),
        in_specs=[pl.BlockSpec(memory_space=pltpu.HBM)] * 8,
        out_specs=[pl.BlockSpec(memory_space=pltpu.VMEM)] * 7,
        scratch_shapes=[
            pltpu.VMEM((pages, PAGE, HEAD), BF16),
            pltpu.SemaphoreType.DMA((8,)),
            pltpu.SemaphoreType.DMA((n_give,)),
            pltpu.SemaphoreType.DMA((n_give,)),
        ]
        + gather_sems(q.shape[0]),
        compiler_params=pltpu.CompilerParams(
            collective_id=0, has_side_effects=True, vmem_limit_bytes=24 * MIB
        ),
        name="exchange",
    )(q, k, v, nk, nv, slots, counts, w)


def write_message(ref, top, total, sums):
    ref[0:HEAD, :] = sums.astype(BF16)
    high = total.astype(BF16).astype(F32)
    low = total - high
    row = lax.broadcasted_iota(jnp.int32, (MSG - HEAD, HALF), 0)
    stats = jnp.where(row == 0, top, jnp.where(row == 1, high, jnp.where(row == 2, low, 0.0)))
    ref[HEAD:MSG, :] = stats.astype(BF16)


def merged(refs):
    tops, totals = [], []
    for ref in refs:
        stats = ref[HEAD:MSG, :].astype(F32)
        tops.append(stats[0:1, :])
        totals.append(stats[1:2, :] + stats[2:3, :])
    top = tops[0]
    for other in tops[1:]:
        top = jnp.maximum(top, other)
    total = None
    sums = None
    for ref, t, n in zip(refs, tops, totals):
        scale = jnp.exp2(t - top)
        piece = ref[0:HEAD, :].astype(F32) * scale
        total = n * scale if total is None else total + n * scale
        sums = piece if sums is None else sums + piece
    return top, total, sums


def partial_kernel(
    slots_ref, counts_ref, q_ref, k_ref, vt_ref, new_ref, out_ref, nvt, lag, earlier, count_of, order
):
    me = lax.axis_index("ctx")
    core = me % 2
    contract = (((1,), (1,)), ((), ()))
    fresh = 2 * QTOK
    rows = 2 * HALF
    nvt[0:HEAD, :] = new_ref[:, 1].reshape(fresh, HEAD).astype(F32).T.astype(BF16)
    nvt[HEAD:MSG, :] = jnp.ones((MSG - HEAD, fresh), BF16)
    key = lax.broadcasted_iota(jnp.int32, (fresh, rows), 0)
    held = jnp.where(key < QTOK, me * QTOK, (me - 2 * core) * QTOK)
    lag[...] = key + held - lax.broadcasted_iota(jnp.int32, (fresh, rows), 1) // GROUP

    counts = [counts_ref[0, 0, 2 * j + core] + counts_ref[1, 0, 2 * j + core] for j in range(COLUMN)]
    for j in range(COLUMN):
        rank = 0
        for i in range(COLUMN):
            if i != j:
                ahead = counts[i] >= counts[j] if i < j else counts[i] > counts[j]
                rank = rank + ahead.astype(jnp.int32)
        order[rank] = j
        count_of[j] = counts[j]

    def attend(slot, n, start):
        b = slot * 2 + core
        own = counts_ref[0, 0, b]
        live_pages = count_of[slot] - start
        q = q_ref[slot].reshape(rows, HEAD)
        new = lax.dot_general(new_ref[:, 0].reshape(fresh, HEAD), q, contract, preferred_element_type=F32)
        live = lag[...] <= jnp.where(start == 0, b * QTOK, -2 * COLUMN * QTOK)
        new = jnp.where(live, new, NEG_FILL)
        top = jnp.max(new, axis=0, keepdims=True)
        scores, values = [], []
        for i in range(n):
            at = start + i
            mine = slots_ref[0, jnp.minimum(at, MOST - 1), b]
            theirs = slots_ref[1, jnp.clip(at - own, 0, MOST - 1), b]
            side = jnp.where(at < own, 0, 1)
            page = jnp.where(at < own, mine, theirs)
            score = lax.dot_general(k_ref[side, page], q, contract, preferred_element_type=F32)
            scores.append(score)
            values.append(vt_ref[side, page])
            most = jnp.max(score, axis=0, keepdims=True)
            top = jnp.maximum(top, jnp.where(i < live_pages, most, NEG_FILL))
        top = (top * FACTOR).astype(BF16).astype(F32)
        weights = jnp.where(live, jnp.exp2(new * FACTOR - top), 0.0).astype(BF16)
        both = jnp.dot(nvt[...], weights, preferred_element_type=F32)
        if n:
            weights = [
                jnp.exp2(s * FACTOR - jnp.where(i < live_pages, top, -NEG_FILL)).astype(BF16)
                for i, s in enumerate(scores)
            ]
            both = both + jnp.dot(
                jnp.concatenate(values, axis=1), jnp.concatenate(weights, axis=0), preferred_element_type=F32
            )
        return top, both

    def run_case(slots, n, start):
        for slot, (top, both) in [(s, attend(s, n, start)) for s in slots]:
            for half in HALVES:
                cols = slice(half * HALF, (half + 1) * HALF)
                write_message(
                    out_ref.at[slot, half], top[:, cols], both[HEAD : HEAD + 1, cols], both[0:HEAD, cols]
                )

    def team(i, _):
        slots = [order[i * TEAM + j] for j in range(TEAM)]
        steps = (jnp.minimum(count_of[slots[0]], MOST) + 1) // 2
        for n in range(0, MOST + 1, 2):
            pl.when(steps == n // 2)(functools.partial(run_case, slots, n, 0))
        return 0

    lax.fori_loop(0, COLUMN // TEAM, team, 0)

    def more(i, _):
        slot = order[i]
        earlier[...] = out_ref[slot]
        steps = (count_of[slot] - MOST + 1) // 2
        for n in range(2, MOST + 1, 2):
            pl.when(steps == n // 2)(functools.partial(run_case, [slot], n, MOST))
        for half in HALVES:
            write_message(out_ref.at[slot, half], *merged([out_ref.at[slot, half], earlier.at[half]]))
        return 0

    busy = 0
    for count in counts:
        busy = busy + (count > MOST).astype(jnp.int32)
    lax.fori_loop(0, busy, more, 0)


def partials(slots, counts, q, k, vt, new):
    return pl.pallas_call(
        partial_kernel,
        out_shape=jax.ShapeDtypeStruct((COLUMN, 2, MSG, HALF), BF16),
        in_specs=[pl.BlockSpec(memory_space=pltpu.SMEM)] * 2 + [pl.BlockSpec(memory_space=pltpu.VMEM)] * 4,
        out_specs=pl.BlockSpec(memory_space=pltpu.VMEM),
        scratch_shapes=[
            pltpu.VMEM((MSG, 2 * QTOK), BF16),
            pltpu.VMEM((2 * QTOK, 2 * HALF), jnp.int32),
            pltpu.VMEM((2, MSG, HALF), BF16),
            pltpu.SMEM((COLUMN,), jnp.int32),
            pltpu.SMEM((COLUMN,), jnp.int32),
        ],
        compiler_params=pltpu.CompilerParams(vmem_limit_bytes=24 * MIB),
        name="partials",
    )(slots, counts, q, k, vt, new)


def finish_kernel(
    p_ref, w_ref, out_ref,
    t_buf, r_buf, y_buf, turned, a_buf, mine_buf, kv_buf,
    rz_send, rz_recv, ry_send, ry_recv, kv_send, kv_recv, *sems,
):
    place = Place()
    peers = [dict(ctx=where) for where in place.neighbours(False)]
    for off in range(1, ZS):
        other = lax.rem(place.kv + off, ZS)
        peers += [dict(kv=other), dict(ctx=place.sibling, kv=other)]
    greet(peers)

    def mine(dz, chain, half):
        return p_ref.at[place.slot(dz, chain), half]

    def fold_to(chain, way, left, half):
        at = chain, way, left - 1, half
        entry = left == FAR or (left == FAR - 1 and isinstance(way, int) and way != half)
        src = mine(sign(way) * left, chain, half) if entry else t_buf.at[at]
        target = place.block(sign(way), chain if left == 1 else 0)
        return remote(src, r_buf.at[at], rz_send.at[at], rz_recv.at[at], ctx=target)

    def fold_from(chain, way, left, half):
        at = chain, way, left - 1, half
        remote(r_buf.at[at], r_buf.at[at], rz_send.at[at], rz_recv.at[at], ctx=place.partner).wait_recv()
        return r_buf.at[at]

    def fold(chain, way, left, half):
        parts = [mine(sign(way) * left, chain, half), fold_from(chain, way, left + 1, half)]
        write_message(t_buf.at[chain, way, left - 1, half], *merged(parts))
        fold_to(chain, way, left, half).start()

    def y_copy(half):
        return remote(
            mine(0, 1, half), y_buf.at[half], ry_send.at[half], ry_recv.at[half], ctx=place.partner
        )

    for half in HALVES:
        for chain in (1, 0):
            fold_to(chain, half, FAR, half).start()
    for half in HALVES:
        for chain in (1, 0):
            fold_to(chain, 1 - half, FAR - 1, half).start()
    for half in HALVES:
        y_copy(half).start()
    for half in HALVES:
        for chain in (1, 0):
            fold(chain, half, FAR - 1, half)
    for left in (2, 1):
        for half in HALVES:
            for chain in (1, 0):
                for way in place.ways():
                    fold(chain, way, left, half)

    here = place.slot(0, 0)
    gather = Gather(place, a_buf, lambda half: a_buf.at[here, half], False, *sems)
    for half in HALVES:
        parts = [mine(0, 0, half)]
        for chain in (1, 0):
            for way in (0, 1):
                parts.append(fold_from(chain, way, 1, half))
        remote(y_buf.at[half], y_buf.at[half], ry_send.at[half], ry_recv.at[half], ctx=place.partner).wait_recv()
        _, total, sums = merged(parts + [y_buf.at[half]])
        turned[half] = (sums * (1.0 / total)).T
        tokens = QTOK // 2
        for g in range(GROUP):
            a_buf[here, half, :, g * HEAD : (g + 1) * HEAD] = turned[
                half, pl.ds(g, tokens, stride=GROUP), :
            ].astype(BF16)
        gather.start(half)
    gather.start_across()

    width = w_ref.shape[2]

    def project(dz):
        plane = lax.rem(place.z + dz + ZS, ZS)
        rows = a_buf[pl.ds(plane * 2, 2)].reshape(2 * QTOK, a_buf.shape[3])
        for side in (0, 1):
            done = jnp.dot(rows, w_ref[side], preferred_element_type=F32)
            mine_buf[plane, side] = done.astype(BF16)

        def copy(side, **where):
            return remote(
                mine_buf.at[plane, side], kv_buf.at[place.kv, side],
                kv_send.at[plane, side], kv_recv.at[place.kv, side], **where,
            )

        @pl.when(plane != place.kv)
        def _():
            copy(0, kv=plane).start()
            copy(1, ctx=place.sibling, kv=plane).start()

        @pl.when(plane == place.kv)
        def _():
            copy(1, ctx=place.sibling).start()

    for step in range(1, FAR):
        for chain in (0, 1):
            gather.hop(chain, step)
        if step == 1:
            gather.wait_across()
            project(0)
        else:
            project(step - 1)
            project(1 - step)
    project(FAR - 1)
    project(1 - FAR)
    for chain in (0, 1):
        gather.hop(chain, FAR)
    project(FAR)

    totals = [mine_buf[place.kv, 0].astype(F32), None]
    for off in range(ZS):
        other = lax.rem(place.kv + off, ZS)
        for side in (0, 1):
            if off == 0 and side == 0:
                continue
            where = dict(kv=other) if side == 0 else dict(ctx=place.sibling, kv=other)
            remote(
                mine_buf.at[other, side], kv_buf.at[other, side],
                kv_send.at[other, side], kv_recv.at[other, side], **where,
            ).wait()
            piece = kv_buf[other, side].astype(F32)
            totals[side] = piece if totals[side] is None else totals[side] + piece
    for side in (0, 1):
        core = place.core if side == 0 else 1 - place.core
        done = totals[side].astype(BF16).reshape(2, QTOK, width)
        for yh in (0, 1):
            out_ref[pl.ds(pl.multiple_of(yh * 2 * QTOK + core * QTOK, QTOK), QTOK), :] = done[yh]
    for half in HALVES:
        y_copy(half).wait_send()
        for chain in (0, 1):
            for left in range(1, FAR + 1):
                for way in (0, 1) if left < FAR else (half,):
                    fold_to(chain, way, left, half).wait_send()
    gather.finish()


def finish(p, w):
    depth, width = w.shape[1:]
    return pl.pallas_call(
        finish_kernel,
        out_shape=jax.ShapeDtypeStruct((4 * QTOK, width), BF16),
        in_specs=[pl.BlockSpec(memory_space=pltpu.VMEM)] * 2,
        out_specs=pl.BlockSpec(memory_space=pltpu.VMEM),
        scratch_shapes=[
            pltpu.VMEM((2, 2, 4, 2, MSG, HALF), BF16),
            pltpu.VMEM((2, 2, 4, 2, MSG, HALF), BF16),
            pltpu.VMEM((2, MSG, HALF), BF16),
            pltpu.VMEM((2, HALF, HEAD), F32),
            pltpu.VMEM((COLUMN, 2, QTOK // 2, depth), BF16),
            pltpu.VMEM((ZS, 2, 2 * QTOK, width), BF16),
            pltpu.VMEM((ZS, 2, 2 * QTOK, width), BF16),
            pltpu.SemaphoreType.DMA((2, 2, 4, 2)),
            pltpu.SemaphoreType.DMA((2, 2, 4, 2)),
            pltpu.SemaphoreType.DMA((2,)),
            pltpu.SemaphoreType.DMA((2,)),
            pltpu.SemaphoreType.DMA((ZS, 2)),
            pltpu.SemaphoreType.DMA((ZS, 2)),
        ]
        + gather_sems(2),
        compiler_params=pltpu.CompilerParams(
            collective_id=1, has_side_effects=True, vmem_limit_bytes=24 * MIB
        ),
        name="finish",
    )(p, w)


def body(queries, new_keys, new_values, key_cache, value_cache, page_slots, page_counts, out_weight):
    q = queries.reshape(Q_PIECES, 2 * HALF // Q_PIECES, HEAD)
    nk = new_keys.reshape(QTOK, HEAD)
    nv = new_values.reshape(QTOK, HEAD)
    k = key_cache.reshape(-1, PAGE, HEAD)
    v = value_cache.reshape(-1, PAGE, HEAD)
    arrays = q, k, v, nk, nv, page_slots[0].T, page_counts, out_weight
    q_all, k_all, vt_all, new_all, slots, counts, w_all = exchange(
        *(pltpu.with_memory_space_constraint(array, pltpu.HBM) for array in arrays)
    )
    p = partials(slots, counts, q_all, k_all, vt_all, new_all)
    return finish(p, w_all)


def solution(mesh):
    placed = (
        P("ctx", "kv", None),
        P("ctx", "kv", None),
        P("ctx", "kv", None),
        P("ctx", "kv", None),
        P("ctx", "kv", None),
        P("ctx", None, None),
        P("ctx", None),
        P("kv", "ctx"),
    )
    return jax.shard_map(
        body, mesh=mesh, in_specs=placed, out_specs=P("kv", "ctx"), check_vma=False
    )
```

```python
import functools

import jax
import jax.numpy as jnp
from jax import lax
from jax.experimental import pallas as pl
from jax.experimental.pallas import tpu as pltpu
from jax.sharding import PartitionSpec as P

PAGE = 128
HEAD = 128
QTOK = 32
GROUP = 8
HALF = 128
MSG = 144
ZS = 8
COLUMN = 16
MOST = 8
TEAM = 4
NEG_FILL = -1e30
FACTOR = HEAD ** (-0.5) * 1.4426950408889634
MIB = 1 << 20
MESH = pl.DeviceIdType.MESH
BF16 = jnp.bfloat16
F32 = jnp.float32

WAYS = (1, -1)
HALVES = (0, 1)
FAR = 4
Q_PIECES = 2


class Place:
    def __init__(self):
        self.me = lax.axis_index("ctx")
        self.kv = lax.axis_index("kv")
        self.z = self.me // 4
        self.yh = (self.me % 4) // 2
        self.core = self.me % 2
        self.partner = self.block(0, 1)
        self.sibling = self.z * 4 + self.yh * 2 + 1 - self.core
        self.first = jnp.where(self.z % 4 < 2, 1, 0)

    def neighbours(self, jump):
        near = [self.block(dz, chain) for chain in (0, 1) for dz in WAYS]
        return near + [self.block(2 * dz, 0) for dz in WAYS if jump] + [self.partner, self.sibling]

    def slot(self, dz, chain):
        z = lax.rem(self.z + dz + ZS, ZS)
        return z * 2 + (1 - self.yh if chain else self.yh)

    def block(self, dz, chain):
        return self.slot(dz, chain) * 2 + self.core

    def ways(self):
        return self.first, 1 - self.first


def remote(src, dst, send, recv, **where):
    return pltpu.make_async_remote_copy(
        src_ref=src, dst_ref=dst, send_sem=send, recv_sem=recv, device_id=where, device_id_type=MESH
    )


def greet(wheres):
    barrier = pltpu.get_barrier_semaphore()
    for where in wheres:
        pl.semaphore_signal(barrier, inc=1, device_id=where, device_id_type=MESH)
    pl.semaphore_wait(barrier, len(wheres))


def sign(way):
    return 1 - 2 * way


class Gather:
    def __init__(self, place, slots, own, leap, z_send, z_recv, y_send, y_recv):
        self.place, self.slots, self.own, self.leap = place, slots, own, leap
        self.z_send, self.z_recv, self.y_send, self.y_recv = z_send, z_recv, y_send, y_recv
        self.pieces = range(slots.shape[1])

    def hop_to(self, chain, way, step, piece):
        at = chain, way, step - 1, piece
        jump = 2 if step == FAR and self.leap else 1
        if step == 1:
            src, dst = self.own(piece), self.slots.at[self.place.slot(0, 0), piece]
        else:
            src = dst = self.slots.at[self.place.slot((jump - step) * sign(way), chain), piece]
        target = self.place.block(jump * sign(way), chain if step == 1 else 0)
        return remote(src, dst, self.z_send.at[at], self.z_recv.at[at], ctx=target)

    def hop_from(self, chain, way, step, piece):
        at = chain, way, step - 1, piece
        there = self.slots.at[self.place.slot(-step * sign(way), chain), piece]
        return remote(there, there, self.z_send.at[at], self.z_recv.at[at], ctx=self.place.partner)

    def across(self, piece):
        dst = self.slots.at[self.place.slot(0, 0), piece]
        return remote(self.own(piece), dst, self.y_send.at[piece], self.y_recv.at[piece], ctx=self.place.partner)

    def start(self, piece):
        for chain in (0, 1):
            for way in (0, 1):
                self.hop_to(chain, way, 1, piece).start()

    def start_across(self):
        for piece in self.pieces:
            self.across(piece).start()

    def wait_across(self):
        for piece in self.pieces:
            there = self.slots.at[self.place.slot(0, 1), piece]
            remote(
                there, there, self.y_send.at[piece], self.y_recv.at[piece], ctx=self.place.partner
            ).wait_recv()

    def hop(self, chain, step, between=None):
        for piece in self.pieces:
            far = piece % 2
            if between is not None:
                between()
            if step == FAR:
                self.hop_from(chain, far, step, piece).wait_recv()
                continue
            for way in self.place.ways():
                self.hop_from(chain, way, step, piece).wait_recv()
                if step == FAR - (2 if self.leap else 1):
                    pl.when(way == far)(self.hop_to(chain, way, FAR, piece).start)
                if step < FAR - 1:
                    self.hop_to(chain, way, step + 1, piece).start()

    def finish(self):
        for piece in self.pieces:
            self.across(piece).wait_send()
            for chain in (0, 1):
                for step in range(1, FAR + 1):
                    for way in (0, 1) if step < FAR else (piece % 2,):
                        self.hop_to(chain, way, step, piece).wait_send()


def gather_sems(pieces):
    return [
        pltpu.SemaphoreType.DMA((2, 2, FAR, pieces)),
        pltpu.SemaphoreType.DMA((2, 2, FAR, pieces)),
        pltpu.SemaphoreType.DMA((pieces,)),
        pltpu.SemaphoreType.DMA((pieces,)),
    ]


def exchange_kernel(
    q_ref, k_ref, v_ref, nk_ref, nv_ref, slots_ref, counts_ref, w_ref,
    g_out, k_out, vt_out, new_out, slots_out, counts_out, w_out,
    v_buf, l_sem, c_send, c_recv, *sems,
):
    place = Place()
    pages = v_buf.shape[0]
    local = [
        pltpu.make_async_copy(src, dst, l_sem.at[i])
        for i, (src, dst) in enumerate(
            (
                (v_ref, v_buf),
                (k_ref, k_out.at[0]),
                (q_ref, g_out.at[place.slot(0, 0)]),
                (nk_ref, new_out.at[0, 0]),
                (nv_ref, new_out.at[0, 1]),
                (slots_ref, slots_out.at[0]),
                (counts_ref, counts_out.at[0]),
                (w_ref, w_out.at[0]),
            )
        )
    ]
    for copy in local:
        copy.start()
    greet([dict(ctx=where) for where in place.neighbours(True)])

    gather = Gather(place, g_out, lambda piece: q_ref.at[piece], True, *sems)
    for piece in gather.pieces:
        gather.start(piece)
    gather.start_across()

    to_sibling = []

    def give(src, dst):
        i = len(to_sibling)
        copy = remote(src, dst, c_send.at[i], c_recv.at[i], ctx=place.sibling)
        copy.start()
        to_sibling.append(copy)

    give(slots_ref, slots_out.at[1])
    give(counts_ref, counts_out.at[1])
    give(nk_ref, new_out.at[1, 0])
    give(nv_ref, new_out.at[1, 1])
    quarter = pages // 4
    for i in range(4):
        part = pl.ds(i * quarter, quarter)
        give(k_ref.at[part], k_out.at[1, part])
    give(w_ref, w_out.at[1])

    todo = list(range(16))
    each = pages // 16

    def between():
        if not todo:
            return
        i = todo.pop(0)
        if i == 0:
            local[0].wait()

        def turn(p, _):
            vt_out[0, p, 0:HEAD, :] = v_buf[p].T
            vt_out[0, p, HEAD:MSG, :] = jnp.ones((MSG - HEAD, PAGE), BF16)
            vt_out[1, p, HEAD:MSG, :] = jnp.ones((MSG - HEAD, PAGE), BF16)
            return 0

        lax.fori_loop(i * each, (i + 1) * each, turn, 0)
        if i % 4 == 3:
            part = pl.ds((i - 3) * each, 4 * each), pl.ds(0, HEAD)
            give(vt_out.at[(0,) + part], vt_out.at[(1,) + part])

    for _ in range(8):
        between()
    for step in range(1, FAR):
        for chain in (0, 1):
            gather.hop(chain, step, between)
    while todo:
        between()
    for chain in (0, 1):
        gather.hop(chain, FAR)
    gather.wait_across()
    gather.finish()
    for copy in local[1:]:
        copy.wait()
    for copy in to_sibling:
        copy.wait()


def exchange(q, k, v, nk, nv, slots, counts, w):
    pages = v.shape[0]
    n_give = 13
    return pl.pallas_call(
        exchange_kernel,
        out_shape=(
            jax.ShapeDtypeStruct((COLUMN,) + q.shape, BF16),
            jax.ShapeDtypeStruct((2, pages, PAGE, HEAD), BF16),
            jax.ShapeDtypeStruct((2, pages, MSG, PAGE), BF16),
            jax.ShapeDtypeStruct((2, 2, QTOK, HEAD), BF16),
            jax.ShapeDtypeStruct((2,) + slots.shape, jnp.int32),
            jax.ShapeDtypeStruct((2,) + counts.shape, jnp.int32),
            jax.ShapeDtypeStruct((2,) + w.shape, BF16),
        ),
        in_specs=[pl.BlockSpec(memory_space=pltpu.HBM)] * 8,
        out_specs=[pl.BlockSpec(memory_space=pltpu.VMEM)] * 7,
        scratch_shapes=[
            pltpu.VMEM((pages, PAGE, HEAD), BF16),
            pltpu.SemaphoreType.DMA((8,)),
            pltpu.SemaphoreType.DMA((n_give,)),
            pltpu.SemaphoreType.DMA((n_give,)),
        ]
        + gather_sems(q.shape[0]),
        compiler_params=pltpu.CompilerParams(
            collective_id=0, has_side_effects=True, vmem_limit_bytes=24 * MIB
        ),
        name="exchange",
    )(q, k, v, nk, nv, slots, counts, w)


def write_message(ref, top, total, sums):
    ref[0:HEAD, :] = sums.astype(BF16)
    high = total.astype(BF16).astype(F32)
    low = total - high
    row = lax.broadcasted_iota(jnp.int32, (MSG - HEAD, HALF), 0)
    stats = jnp.where(row == 0, top, jnp.where(row == 1, high, jnp.where(row == 2, low, 0.0)))
    ref[HEAD:MSG, :] = stats.astype(BF16)


def merged(refs):
    tops, totals = [], []
    for ref in refs:
        stats = ref[HEAD:MSG, :].astype(F32)
        tops.append(stats[0:1, :])
        totals.append(stats[1:2, :] + stats[2:3, :])
    top = tops[0]
    for other in tops[1:]:
        top = jnp.maximum(top, other)
    total = None
    sums = None
    for ref, t, n in zip(refs, tops, totals):
        scale = jnp.exp2(t - top)
        piece = ref[0:HEAD, :].astype(F32) * scale
        total = n * scale if total is None else total + n * scale
        sums = piece if sums is None else sums + piece
    return top, total, sums


def partial_kernel(
    slots_ref, counts_ref, q_ref, k_ref, vt_ref, new_ref, out_ref, nvt, lag, earlier, count_of, order
):
    me = lax.axis_index("ctx")
    core = me % 2
    contract = (((1,), (1,)), ((), ()))
    fresh = 2 * QTOK
    rows = 2 * HALF
    nvt[0:HEAD, :] = new_ref[:, 1].reshape(fresh, HEAD).astype(F32).T.astype(BF16)
    nvt[HEAD:MSG, :] = jnp.ones((MSG - HEAD, fresh), BF16)
    key = lax.broadcasted_iota(jnp.int32, (fresh, rows), 0)
    held = jnp.where(key < QTOK, me * QTOK, (me - 2 * core) * QTOK)
    lag[...] = key + held - lax.broadcasted_iota(jnp.int32, (fresh, rows), 1) // GROUP

    counts = [counts_ref[0, 0, 2 * j + core] + counts_ref[1, 0, 2 * j + core] for j in range(COLUMN)]
    for j in range(COLUMN):
        rank = 0
        for i in range(COLUMN):
            if i != j:
                ahead = counts[i] >= counts[j] if i < j else counts[i] > counts[j]
                rank = rank + ahead.astype(jnp.int32)
        order[rank] = j
        count_of[j] = counts[j]

    def attend(slot, n, start):
        b = slot * 2 + core
        own = counts_ref[0, 0, b]
        live_pages = count_of[slot] - start
        q = q_ref[slot].reshape(rows, HEAD)
        new = lax.dot_general(new_ref[:, 0].reshape(fresh, HEAD), q, contract, preferred_element_type=F32)
        live = lag[...] <= jnp.where(start == 0, b * QTOK, -2 * COLUMN * QTOK)
        new = jnp.where(live, new, NEG_FILL)
        top = jnp.max(new, axis=0, keepdims=True)
        scores, values = [], []
        for i in range(n):
            at = start + i
            mine = slots_ref[0, jnp.minimum(at, MOST - 1), b]
            theirs = slots_ref[1, jnp.clip(at - own, 0, MOST - 1), b]
            side = jnp.where(at < own, 0, 1)
            page = jnp.where(at < own, mine, theirs)
            score = lax.dot_general(k_ref[side, page], q, contract, preferred_element_type=F32)
            scores.append(score)
            values.append(vt_ref[side, page])
            most = jnp.max(score, axis=0, keepdims=True)
            top = jnp.maximum(top, jnp.where(i < live_pages, most, NEG_FILL))
        top = (top * FACTOR).astype(BF16).astype(F32)
        weights = jnp.where(live, jnp.exp2(new * FACTOR - top), 0.0).astype(BF16)
        both = jnp.dot(nvt[...], weights, preferred_element_type=F32)
        if n:
            weights = [
                jnp.exp2(s * FACTOR - jnp.where(i < live_pages, top, -NEG_FILL)).astype(BF16)
                for i, s in enumerate(scores)
            ]
            both = both + jnp.dot(
                jnp.concatenate(values, axis=1), jnp.concatenate(weights, axis=0), preferred_element_type=F32
            )
        return top, both

    def run_case(slots, n, start):
        for slot, (top, both) in [(s, attend(s, n, start)) for s in slots]:
            for half in HALVES:
                cols = slice(half * HALF, (half + 1) * HALF)
                write_message(
                    out_ref.at[slot, half], top[:, cols], both[HEAD : HEAD + 1, cols], both[0:HEAD, cols]
                )

    def team(i, _):
        slots = [order[i * TEAM + j] for j in range(TEAM)]
        steps = (jnp.minimum(count_of[slots[0]], MOST) + 1) // 2
        for n in range(0, MOST + 1, 2):
            pl.when(steps == n // 2)(functools.partial(run_case, slots, n, 0))
        return 0

    lax.fori_loop(0, COLUMN // TEAM, team, 0)

    def more(i, _):
        slot = order[i]
        earlier[...] = out_ref[slot]
        steps = (count_of[slot] - MOST + 1) // 2
        for n in range(2, MOST + 1, 2):
            pl.when(steps == n // 2)(functools.partial(run_case, [slot], n, MOST))
        for half in HALVES:
            write_message(out_ref.at[slot, half], *merged([out_ref.at[slot, half], earlier.at[half]]))
        return 0

    busy = 0
    for count in counts:
        busy = busy + (count > MOST).astype(jnp.int32)
    lax.fori_loop(0, busy, more, 0)


def partials(slots, counts, q, k, vt, new):
    return pl.pallas_call(
        partial_kernel,
        out_shape=jax.ShapeDtypeStruct((COLUMN, 2, MSG, HALF), BF16),
        in_specs=[pl.BlockSpec(memory_space=pltpu.SMEM)] * 2 + [pl.BlockSpec(memory_space=pltpu.VMEM)] * 4,
        out_specs=pl.BlockSpec(memory_space=pltpu.VMEM),
        scratch_shapes=[
            pltpu.VMEM((MSG, 2 * QTOK), BF16),
            pltpu.VMEM((2 * QTOK, 2 * HALF), jnp.int32),
            pltpu.VMEM((2, MSG, HALF), BF16),
            pltpu.SMEM((COLUMN,), jnp.int32),
            pltpu.SMEM((COLUMN,), jnp.int32),
        ],
        compiler_params=pltpu.CompilerParams(vmem_limit_bytes=24 * MIB),
        name="partials",
    )(slots, counts, q, k, vt, new)


def finish_kernel(
    p_ref, w_ref, out_ref,
    t_buf, r_buf, y_buf, turned, a_buf, mine_buf, kv_buf,
    rz_send, rz_recv, ry_send, ry_recv, kv_send, kv_recv, *sems,
):
    place = Place()
    peers = [dict(ctx=where) for where in place.neighbours(False)]
    for off in range(1, ZS):
        other = lax.rem(place.kv + off, ZS)
        peers += [dict(kv=other), dict(ctx=place.sibling, kv=other)]
    greet(peers)

    def mine(dz, chain, half):
        return p_ref.at[place.slot(dz, chain), half]

    def fold_to(chain, way, left, half):
        at = chain, way, left - 1, half
        entry = left == FAR or (left == FAR - 1 and isinstance(way, int) and way != half)
        src = mine(sign(way) * left, chain, half) if entry else t_buf.at[at]
        target = place.block(sign(way), chain if left == 1 else 0)
        return remote(src, r_buf.at[at], rz_send.at[at], rz_recv.at[at], ctx=target)

    def fold_from(chain, way, left, half):
        at = chain, way, left - 1, half
        remote(r_buf.at[at], r_buf.at[at], rz_send.at[at], rz_recv.at[at], ctx=place.partner).wait_recv()
        return r_buf.at[at]

    def fold(chain, way, left, half):
        parts = [mine(sign(way) * left, chain, half), fold_from(chain, way, left + 1, half)]
        write_message(t_buf.at[chain, way, left - 1, half], *merged(parts))
        fold_to(chain, way, left, half).start()

    def y_copy(half):
        return remote(
            mine(0, 1, half), y_buf.at[half], ry_send.at[half], ry_recv.at[half], ctx=place.partner
        )

    for half in HALVES:
        for chain in (1, 0):
            fold_to(chain, half, FAR, half).start()
    for half in HALVES:
        for chain in (1, 0):
            fold_to(chain, 1 - half, FAR - 1, half).start()
    for half in HALVES:
        y_copy(half).start()
    for half in HALVES:
        for chain in (1, 0):
            fold(chain, half, FAR - 1, half)
    for left in (2, 1):
        for half in HALVES:
            for chain in (1, 0):
                for way in place.ways():
                    fold(chain, way, left, half)

    here = place.slot(0, 0)
    gather = Gather(place, a_buf, lambda half: a_buf.at[here, half], False, *sems)
    for half in HALVES:
        parts = [mine(0, 0, half)]
        for chain in (1, 0):
            for way in (0, 1):
                parts.append(fold_from(chain, way, 1, half))
        remote(y_buf.at[half], y_buf.at[half], ry_send.at[half], ry_recv.at[half], ctx=place.partner).wait_recv()
        _, total, sums = merged(parts + [y_buf.at[half]])
        turned[half] = (sums * (1.0 / total)).T
        tokens = QTOK // 2
        for g in range(GROUP):
            a_buf[here, half, :, g * HEAD : (g + 1) * HEAD] = turned[
                half, pl.ds(g, tokens, stride=GROUP), :
            ].astype(BF16)
        gather.start(half)
    gather.start_across()

    width = w_ref.shape[2]

    def project(*dzs):
        planes = [lax.rem(place.z + dz + ZS, ZS) for dz in dzs]
        rows = [a_buf[pl.ds(plane * 2, 2)].reshape(2 * QTOK, a_buf.shape[3]) for plane in planes]
        rows = jnp.concatenate(rows, axis=0) if len(rows) > 1 else rows[0]
        for side in (0, 1):
            done = jnp.dot(rows, w_ref[side], preferred_element_type=F32).astype(BF16)
            for i, plane in enumerate(planes):
                mine_buf[plane, side] = done[i * 2 * QTOK : (i + 1) * 2 * QTOK]
        for plane in planes:
            hand_out(plane)

    def hand_out(plane):

        def copy(side, **where):
            return remote(
                mine_buf.at[plane, side], kv_buf.at[place.kv, side],
                kv_send.at[plane, side], kv_recv.at[place.kv, side], **where,
            )

        @pl.when(plane != place.kv)
        def _():
            copy(0, kv=plane).start()
            copy(1, ctx=place.sibling, kv=plane).start()

        @pl.when(plane == place.kv)
        def _():
            copy(1, ctx=place.sibling).start()

    for step in range(1, FAR):
        for chain in (0, 1):
            gather.hop(chain, step)
        if step == 1:
            gather.wait_across()
            project(0)
        else:
            project(step - 1, 1 - step)
    project(FAR - 1, 1 - FAR)
    for chain in (0, 1):
        gather.hop(chain, FAR)
    project(FAR)

    totals = [mine_buf[place.kv, 0].astype(F32), None]
    for off in range(ZS):
        other = lax.rem(place.kv + off, ZS)
        for side in (0, 1):
            if off == 0 and side == 0:
                continue
            where = dict(kv=other) if side == 0 else dict(ctx=place.sibling, kv=other)
            remote(
                mine_buf.at[other, side], kv_buf.at[other, side],
                kv_send.at[other, side], kv_recv.at[other, side], **where,
            ).wait()
            piece = kv_buf[other, side].astype(F32)
            totals[side] = piece if totals[side] is None else totals[side] + piece
    for side in (0, 1):
        core = place.core if side == 0 else 1 - place.core
        done = totals[side].astype(BF16).reshape(2, QTOK, width)
        for yh in (0, 1):
            out_ref[pl.ds(pl.multiple_of(yh * 2 * QTOK + core * QTOK, QTOK), QTOK), :] = done[yh]
    for half in HALVES:
        y_copy(half).wait_send()
        for chain in (0, 1):
            for left in range(1, FAR + 1):
                for way in (0, 1) if left < FAR else (half,):
                    fold_to(chain, way, left, half).wait_send()
    gather.finish()


def finish(p, w):
    depth, width = w.shape[1:]
    return pl.pallas_call(
        finish_kernel,
        out_shape=jax.ShapeDtypeStruct((4 * QTOK, width), BF16),
        in_specs=[pl.BlockSpec(memory_space=pltpu.VMEM)] * 2,
        out_specs=pl.BlockSpec(memory_space=pltpu.VMEM),
        scratch_shapes=[
            pltpu.VMEM((2, 2, 4, 2, MSG, HALF), BF16),
            pltpu.VMEM((2, 2, 4, 2, MSG, HALF), BF16),
            pltpu.VMEM((2, MSG, HALF), BF16),
            pltpu.VMEM((2, HALF, HEAD), F32),
            pltpu.VMEM((COLUMN, 2, QTOK // 2, depth), BF16),
            pltpu.VMEM((ZS, 2, 2 * QTOK, width), BF16),
            pltpu.VMEM((ZS, 2, 2 * QTOK, width), BF16),
            pltpu.SemaphoreType.DMA((2, 2, 4, 2)),
            pltpu.SemaphoreType.DMA((2, 2, 4, 2)),
            pltpu.SemaphoreType.DMA((2,)),
            pltpu.SemaphoreType.DMA((2,)),
            pltpu.SemaphoreType.DMA((ZS, 2)),
            pltpu.SemaphoreType.DMA((ZS, 2)),
        ]
        + gather_sems(2),
        compiler_params=pltpu.CompilerParams(
            collective_id=1, has_side_effects=True, vmem_limit_bytes=24 * MIB
        ),
        name="finish",
    )(p, w)


def body(queries, new_keys, new_values, key_cache, value_cache, page_slots, page_counts, out_weight):
    q = queries.reshape(Q_PIECES, 2 * HALF // Q_PIECES, HEAD)
    nk = new_keys.reshape(QTOK, HEAD)
    nv = new_values.reshape(QTOK, HEAD)
    k = key_cache.reshape(-1, PAGE, HEAD)
    v = value_cache.reshape(-1, PAGE, HEAD)
    arrays = q, k, v, nk, nv, page_slots[0].T, page_counts, out_weight
    q_all, k_all, vt_all, new_all, slots, counts, w_all = exchange(
        *(pltpu.with_memory_space_constraint(array, pltpu.HBM) for array in arrays)
    )
    p = partials(slots, counts, q_all, k_all, vt_all, new_all)
    return finish(p, w_all)


def solution(mesh):
    placed = (
        P("ctx", "kv", None),
        P("ctx", "kv", None),
        P("ctx", "kv", None),
        P("ctx", "kv", None),
        P("ctx", "kv", None),
        P("ctx", None, None),
        P("ctx", None),
        P("kv", "ctx"),
    )
    return jax.shard_map(
        body, mesh=mesh, in_specs=placed, out_specs=P("kv", "ctx"), check_vma=False
    )
```
